32 devices in a mesh: pipe: 4 (over y, core), expert: 8 (over z, x).
Axes of the slice: x: 2, y: 2, z: 4, core: 2. Of those that a mesh axis runs over, the one named last changes fastest.
Arguments:
- east_batch: bfloat16 [4, 256, 7168], P('pipe', 'expert'), may hold values from -6 to 6
- west_batch: bfloat16 [4, 256, 7168], P('pipe', 'expert'), may hold values from -6 to 6
- east_entering: bfloat16 [1, 256, 7168], P(None, 'expert'), may hold values from -6 to 6
- west_entering: bfloat16 [1, 256, 7168], P(None, 'expert'), may hold values from -6 to 6
- east_experts: int32 [2, 4, 256, 2], P(None, 'pipe', 'expert'), may hold values from 0 to 3, all different within a row; in each aligned block of 32 rows (0 to 31, 32 to 63, ..., all dimensions but the last counted through in order) at most 18 rows name the same one
- west_experts: int32 [2, 4, 256, 2], P(None, 'pipe', 'expert'), may hold values from 0 to 3, all different within a row; in each aligned block of 32 rows (0 to 31, 32 to 63, ..., all dimensions but the last counted through in order) at most 18 rows name the same one
- east_gates: float32 [2, 4, 256, 2], P(None, 'pipe', 'expert'), may hold values from 0.1 to 1
- west_gates: float32 [2, 4, 256, 2], P(None, 'pipe', 'expert'), may hold values from 0.1 to 1
- norm_gain: float32 [4, 7168], P('pipe'), may hold values from 0.5 to 1.5
- expert_in: bfloat16 [4, 8, 3584, 2048], P('pipe', 'expert'), may hold values from -0.0625 to 0.0625
- expert_down: bfloat16 [4, 8, 1024, 3584], P('pipe', 'expert'), may hold values from -0.1875 to 0.1875
Outputs:
- east_out: bfloat16 [4, 256, 7168], P('pipe', 'expert')
- west_out: bfloat16 [4, 256, 7168], P('pipe', 'expert')
The draws below stay inside these ranges and needn't reach their ends.
Inputs may be any that keep to these rules, and one draw needn't show every extreme that they name: `east_experts`: the 2 experts of a token differ. In each step and section, the 32 tokens of one device name one expert at most 18 times, a bound that some block reaches. `west_experts`: the 2 experts of a token differ. In each step and section, the 32 tokens of one device name one expert at most 18 times, a bound that some block reaches.
All inputs are finite; a program needn't handle non-finite values.
Results may differ from the reference program's by a relative error of at most 0.007.
Values may be sent and summed in bfloat16 or wider, within the bound.
No kernel may reach another device: no remote copies, remote signals or barrier semaphores. Data moves between devices by JAX's collectives and lax.ppermute only.
A program may use at most 128 MiB of HBM per device.

```python
import math
import jax
import jax.numpy as jnp
import numpy as np
from jax import lax

D = 7168
EXP_HID = 1024
EXPERTS = 4
TOPK = 2
TICKS = 2
TOK_DEV = 32
CAP = 18
GROUP = 2
FEAT = 3584
TOKENS = 256
N_PIPE = 4
N_EXPERT = 8


def level_of(rng, dims, shards, smallest, high):
    def one(dim, parts):
        steps = jax.random.uniform(jax.random.fold_in(jax.random.fold_in(rng, 6), dim), (parts,), jnp.float32, smallest / len(shards), high / len(shards))
        return jnp.repeat(jnp.exp(steps), dims[dim] // parts).reshape((-1,) + (1,) * (len(dims) - dim - 1))

    factor_of = one(*shards[0])
    for cut in shards[1:]:
        factor_of = factor_of * one(*cut)
    return factor_of


def assign_block(stream_key, own, number, rows, number_of, top, most, slope):
    ranking = jax.random.permutation(stream_key, number_of)
    packed, ordinary = load_shares(number_of, rows * top, most, slope, True), load_shares(number_of, rows * top, most, slope, False)
    places = jnp.arange(number_of)

    def named(lengths, turn):
        used = int((lengths > 0).sum())
        fixed = max(1, used // 4)
        moved = fixed + (places - fixed + turn * (used - fixed)) % max(1, number_of - fixed)
        return jnp.zeros((number_of,), jnp.int32).at[ranking[jnp.where(places < fixed, places, moved)]].set(jnp.asarray(lengths, jnp.int32))

    lengths = jnp.where(number % 4 == 0, named(packed, number // 4), named(ordinary, number - number // 4 - 1))
    mixed = jax.random.permutation(jax.random.fold_in(own, 3), number_of)
    giver, sink = mixed[0:number_of // 2 * 2:2], mixed[1:number_of // 2 * 2:2]
    slack = jnp.minimum(lengths[giver] - 1, most - lengths[sink]) // 2
    slack = jnp.where((giver == ranking[0]) | (sink == ranking[0]) | (lengths[sink] == 0), 0, jnp.maximum(slack, 0))
    moved = jax.random.randint(jax.random.fold_in(own, 4), (number_of // 2,), 0, 1 << 20) % (slack + 1)
    lengths = lengths.at[giver].add(-moved).at[sink].add(moved)
    labels = jnp.searchsorted(jnp.cumsum(lengths), jnp.arange(rows * top), side="right").astype(jnp.int32)
    listing = labels.reshape(top, rows).T
    listing = listing[jax.random.permutation(jax.random.fold_in(own, 1), rows)]
    turn = jax.random.randint(jax.random.fold_in(own, 2), (rows, 1), 0, top)
    return jnp.take_along_axis(listing, (jnp.arange(top)[None, :] + turn) % top, axis=1)


def load_shares(number_of, total, reach, slope, full):
    loads = [(1 << 20) // math.isqrt(grade ** slope) + 1 for grade in range(1, number_of + 1)]
    largest = reach if full else min(reach, max(-(-total // number_of), total * loads[0] // sum(loads)))
    least = 1 if total - largest >= number_of - 1 else 0
    holding, rest = [largest] + [least] * (number_of - 1), total - largest - least * (number_of - 1)
    while rest > 0:
        free = [i for i in range(1, number_of) if holding[i] < largest] or [i for i in range(1, number_of) if holding[i] < reach]
        mass, remaining = sum([loads[i] for i in free]), rest
        for i in free:
            extra = min(reach - holding[i], max(1, remaining * loads[i] // mass), rest)
            holding[i] = holding[i] + extra
            rest = rest - extra
    return np.array(holding)


def gaussian(own_key, extent, scale, reach, shards=(), held_as=jnp.bfloat16):
    values = scale * jax.random.normal(own_key, extent, jnp.float32)
    if shards:
        values = values * level_of(own_key, extent, shards, -0.22, 0.18)
    return jnp.clip(values, -reach, reach).astype(held_as)


def setup_inputs(seed: int = 0) -> dict:
    seeds = jax.random.split(jax.random.key(seed), 12)
    east_batch = gaussian(seeds[0], (N_PIPE, TOKENS, D), 1.0, 6.0, ((0, 4), (1, 8)))
    west_batch = gaussian(seeds[1], (N_PIPE, TOKENS, D), 1.0, 6.0, ((0, 4), (1, 8)))
    east_entering = gaussian(seeds[2], (TICKS - 1, TOKENS, D), 1.0, 6.0, ((1, 8),))
    west_entering = gaussian(seeds[3], (TICKS - 1, TOKENS, D), 1.0, 6.0, ((1, 8),))
    east_experts_keys = jax.random.split(jax.random.fold_in(seeds[4], 1), TICKS * N_PIPE * TOKENS // TOK_DEV)
    east_experts_turns = jax.random.permutation(jax.random.fold_in(seeds[4], 3), TICKS * N_PIPE * TOKENS // TOK_DEV)
    east_experts = jax.vmap(lambda own, number: assign_block(jax.random.fold_in(seeds[4], 2), own, number, TOK_DEV, EXPERTS, TOPK, CAP, 2))(east_experts_keys, east_experts_turns).reshape((TICKS, N_PIPE, TOKENS, TOPK))
    west_experts_keys = jax.random.split(jax.random.fold_in(seeds[5], 1), TICKS * N_PIPE * TOKENS // TOK_DEV)
    west_experts_turns = jax.random.permutation(jax.random.fold_in(seeds[5], 3), TICKS * N_PIPE * TOKENS // TOK_DEV)
    west_experts = jax.vmap(lambda own, number: assign_block(jax.random.fold_in(seeds[5], 2), own, number, TOK_DEV, EXPERTS, TOPK, CAP, 2))(west_experts_keys, west_experts_turns).reshape((TICKS, N_PIPE, TOKENS, TOPK))
    east_gates = jnp.clip(0.1 + 0.9 * jax.random.uniform(seeds[6], (TICKS, N_PIPE, TOKENS, TOPK), jnp.float32) ** level_of(seeds[6], (TICKS, N_PIPE, TOKENS, TOPK), ((1, 4), (2, 8)), -0.2, 0.2), 0.1, 1.0)
    west_gates = jnp.clip(0.1 + 0.9 * jax.random.uniform(seeds[7], (TICKS, N_PIPE, TOKENS, TOPK), jnp.float32) ** level_of(seeds[7], (TICKS, N_PIPE, TOKENS, TOPK), ((1, 4), (2, 8)), -0.2, 0.2), 0.1, 1.0)
    norm_gain = jnp.clip(1.0 + 0.1 * jax.random.normal(seeds[8], (N_PIPE, D), jnp.float32), 0.5, 1.5)
    expert_in = gaussian(seeds[9], (N_PIPE, N_EXPERT, FEAT, 2 * EXP_HID), D ** -0.5, 0.0625, ((0, 4), (1, 8)))
    expert_down = gaussian(seeds[10], (N_PIPE, N_EXPERT, EXP_HID, FEAT), EXP_HID ** -0.5, 0.1875, ((0, 4), (1, 8)))
    return {"east_batch": east_batch, "west_batch": west_batch, "east_entering": east_entering, "west_entering": west_entering, "east_experts": east_experts, "west_experts": west_experts, "east_gates": east_gates, "west_gates": west_gates, "norm_gain": norm_gain, "expert_in": expert_in, "expert_down": expert_down}


EPSILON = 1e-06

def expert_layer(micro_batch, chosen, shares, gain_row, expert_in, expert_down):
    values = micro_batch.astype(jnp.float32)
    scale_row = lax.rsqrt(lax.optimization_barrier(jnp.mean(values * values, axis=-1, keepdims=True)) + EPSILON)
    normed = (values * scale_row * gain_row[None, :]).astype(jnp.bfloat16)
    limit = N_EXPERT * CAP
    mixed = jnp.zeros(values.shape, jnp.float32)
    for expert_index in range(EXPERTS):
        hit_mask = chosen == expert_index
        named = lax.optimization_barrier(jnp.sum(hit_mask.astype(jnp.int32), axis=1))
        gate_share = lax.optimization_barrier(jnp.sum(jnp.where(hit_mask, shares, jnp.zeros_like(shares)), axis=1))
        row_order = jnp.argsort(1 - named, stable=True)[:limit]
        gathered = normed[row_order]
        weight_in = expert_in[expert_index * GROUP:(expert_index + 1) * GROUP].reshape(D, 2 * EXP_HID)
        projected = jnp.dot(gathered, weight_in, preferred_element_type=jnp.float32)
        hidden = (jax.nn.silu(projected[:, :EXP_HID]) * projected[:, EXP_HID:]).astype(jnp.bfloat16)
        weight_out = jnp.transpose(expert_down[expert_index * GROUP:(expert_index + 1) * GROUP], (1, 0, 2)).reshape(EXP_HID, D)
        expert_out = jnp.dot(hidden, weight_out, preferred_element_type=jnp.float32).astype(jnp.bfloat16)
        expert_out = lax.optimization_barrier(expert_out).astype(jnp.float32)
        mixed = mixed.at[row_order].add(gate_share[row_order][:, None] * expert_out)
    return (values + mixed).astype(jnp.bfloat16)

def reference(east_batch, west_batch, east_entering, west_entering, east_experts, west_experts, east_gates, west_gates, norm_gain, expert_in, expert_down):
    apply_all = jax.vmap(expert_layer)
    east_now = east_batch
    west_now = west_batch
    for tick_index in range(TICKS):
        east_now = apply_all(east_now, east_experts[tick_index], east_gates[tick_index], norm_gain, expert_in, expert_down)
        west_now = apply_all(west_now, west_experts[tick_index], west_gates[tick_index], norm_gain, expert_in, expert_down)
        if tick_index + 1 < TICKS:
            east_now = jnp.concatenate([east_entering[tick_index][None], east_now[:-1]], axis=0)
            west_now = jnp.concatenate([west_now[1:], west_entering[tick_index][None]], axis=0)
    return (east_now, west_now)
```

```python
import functools

import jax
import jax.numpy as jnp
from jax import lax
from jax.experimental import pallas as pl
from jax.experimental.pallas import tpu as pltpu
from jax.sharding import PartitionSpec as P

EXPERTS = 4
TICKS = 2
CAP = 18


EPSILON = 1e-06


def partner(shard, axis, apart):
    return lax.ppermute(shard, axis, [(i, i ^ 1 << apart) for i in range(lax.axis_size(axis))])


def shifted(block, axis, distance):
    devices = range(lax.axis_size(axis))
    route = [(i - distance, i) for i in devices if i - distance in devices]
    return lax.ppermute(block, axis, route)


def rms_scaled(joined_rows, gain_row):
    values = joined_rows.astype(jnp.float32)
    scale_row = lax.rsqrt(jnp.mean(values * values, axis=-1, keepdims=True) + EPSILON)
    return (values * scale_row * gain_row[None, :]).astype(jnp.bfloat16)


def slot_tables(joined_routes, joined_shares, batch_count, experts, capacity):
    total_rows = joined_routes.shape[0]
    row_count = total_rows // batch_count
    onehot = (
        joined_routes[:, :, None] == jnp.arange(experts, dtype=jnp.int32)[None, None, :]
    ).astype(jnp.int32)
    per_row = jnp.sum(onehot, axis=1).reshape(batch_count, row_count, experts)
    before = (jnp.cumsum(per_row, axis=1) - per_row).reshape(total_rows, experts)
    slot_of = jnp.sum(onehot * before[:, None, :], axis=2)
    offset = jnp.arange(total_rows, dtype=jnp.int32) // row_count * capacity
    slot_of = slot_of + offset[:, None]
    slot_ids = jnp.arange(batch_count * capacity, dtype=jnp.int32)
    slot_hit = (slot_of[:, :, None] == slot_ids[None, None, :]).astype(jnp.float32)
    onehot_float = onehot.astype(jnp.float32)
    placement = jnp.einsum("rke,rkc->ecr", onehot_float, slot_hit, precision=lax.Precision.HIGHEST)
    weighted = jnp.einsum(
        "rke,rkc->rec",
        onehot_float * joined_shares[:, :, None],
        slot_hit,
        precision=lax.Precision.HIGHEST,
    )
    return (placement, weighted)


def halving_sum(partial_value, groups, halved_bits):
    row_count = partial_value.shape[0]
    slice_width = partial_value.shape[1] // (2 * groups)
    holding = partial_value.reshape(row_count, 2, groups, slice_width)
    member_index = lax.axis_index("expert")
    held_count = groups
    for bit_index in range(halved_bits):
        own_bit = member_index >> bit_index & 1
        reshaped = holding.reshape(row_count, 2, held_count // 2, 2, slice_width)
        kept_half = lax.dynamic_index_in_dim(reshaped, own_bit, 3, keepdims=False)
        sent_half = lax.dynamic_index_in_dim(reshaped, 1 - own_bit, 3, keepdims=False)
        holding = kept_half + partner(sent_half, "expert", bit_index)
        held_count = held_count // 2
    holding = holding + partner(holding, "expert", halved_bits)
    return (holding[:, 0], holding[:, 1])


def doubling_gather(own_piece, gathered_bits):
    row_count, held_count, slice_width = own_piece.shape
    holding = own_piece
    member_index = lax.axis_index("expert")
    for bit_index in reversed(range(gathered_bits)):
        own_bit = member_index >> bit_index & 1
        arrived = partner(holding, "expert", bit_index)
        first_half = jnp.where(own_bit == 0, holding, arrived)
        second_half = jnp.where(own_bit == 0, arrived, holding)
        stacked = jnp.stack([first_half, second_half], axis=2)
        holding = stacked.reshape(row_count, -1, slice_width)
    return holding.reshape(row_count, -1)


def expert_layer(batch_list, route_list, share_list, gain_row, weight_in, weight_out):
    batch_count = len(batch_list)
    row_count = batch_list[0].shape[0]
    model_width = batch_list[0].shape[1]
    groups = lax.axis_size("expert") // EXPERTS
    bit_count = groups.bit_length() - 1
    halved_bits = bit_count - 1
    feat_width = model_width // groups
    joined_rows = batch_list[0]
    joined_routes = route_list[0]
    joined_shares = share_list[0]
    normed = rms_scaled(joined_rows, gain_row)
    placement, weighted = slot_tables(joined_routes, joined_shares, batch_count, EXPERTS, CAP)
    total_rows = batch_count * row_count
    normed_split = normed.reshape(total_rows, groups, feat_width)
    outgoing = jnp.einsum(
        "ecr,rwf->ewcf",
        placement.astype(jnp.bfloat16),
        normed_split,
        preferred_element_type=jnp.float32,
    ).astype(jnp.bfloat16)
    outgoing = outgoing.reshape(EXPERTS * groups, batch_count * CAP, feat_width)
    arrived = lax.all_to_all(outgoing, "expert", split_axis=0, concat_axis=0, tiled=True)
    sources, slot_count, block_width = arrived.shape
    flat_rows = arrived.reshape(sources * slot_count, block_width)
    partial_value = jnp.dot(flat_rows, weight_in, preferred_element_type=jnp.float32)
    gate_part, up_part = halving_sum(partial_value, groups, halved_bits)
    own_piece = (jax.nn.silu(gate_part) * up_part).astype(jnp.bfloat16)
    hidden = doubling_gather(own_piece, halved_bits)
    result = jnp.dot(hidden, weight_out, preferred_element_type=jnp.float32).astype(jnp.bfloat16)
    returned = lax.all_to_all(
        result.reshape(sources, slot_count, block_width),
        "expert",
        split_axis=0,
        concat_axis=0,
        tiled=True,
    )
    returned_split = returned.reshape(EXPERTS, groups, batch_count * CAP, feat_width).astype(
        jnp.float32
    )
    mixed = jnp.einsum(
        "rec,ewcf->rwf", weighted, returned_split, precision=lax.Precision.HIGHEST
    ).reshape(total_rows, model_width)
    output = (joined_rows.astype(jnp.float32) + mixed).astype(jnp.bfloat16)
    return [output]


def general_shards(
    east_batch,
    west_batch,
    east_entering,
    west_entering,
    east_experts,
    west_experts,
    east_gates,
    west_gates,
    norm_gain,
    expert_in,
    expert_down,
):
    section_index = lax.axis_index("pipe")
    section_count = lax.axis_size("pipe")
    gain_row = norm_gain[0]
    weight_in = expert_in[0, 0]
    weight_out = expert_down[0, 0]
    east_now = east_batch[0]
    west_now = west_batch[0]
    for tick_index in range(TICKS):
        east_routes = east_experts[tick_index, 0]
        west_routes = west_experts[tick_index, 0]
        east_shares = east_gates[tick_index, 0]
        west_shares = west_gates[tick_index, 0]
        east_now = expert_layer(
            [east_now], [east_routes], [east_shares], gain_row, weight_in, weight_out
        )[0]
        west_now = expert_layer(
            [west_now], [west_routes], [west_shares], gain_row, weight_in, weight_out
        )[0]
        if tick_index + 1 < TICKS:
            moved_east = shifted(east_now, "pipe", 1)
            east_now = jnp.where(section_index == 0, east_entering[tick_index], moved_east)
            moved_west = shifted(west_now, "pipe", -1)
            west_now = jnp.where(
                section_index == section_count - 1, west_entering[tick_index], moved_west
            )
    return (east_now[None], west_now[None])


PARTS = 4
LIMIT = 40 * 2**20


def params(limit=LIMIT):
    return pltpu.CompilerParams(vmem_limit_bytes=limit)


def iota(shape, axis):
    return lax.broadcasted_iota(jnp.int32, shape, axis)


def matmul(a, b):
    return jnp.dot(a, b, preferred_element_type=jnp.float32)


def pack_kernel(rows, me, state, route, *outs_and_scratch):
    outs, (stacked,) = outs_and_scratch[:EXPERTS], outs_and_scratch[EXPERTS:]
    tokens, half = state.shape
    width = half // PARTS
    total = PARTS * tokens
    slots = 2 * CAP
    for part in range(PARTS):
        stacked[part * tokens:(part + 1) * tokens, :] = state[:, part * width:(part + 1) * width]
    expert = me[0] ^ iota((8, total), 0)
    named = (route[0:1, :] == expert) | (route[1:2, :] == expert)
    earlier = (iota((total, total), 0) // rows == iota((total, total), 1) // rows) & (
        iota((total, total), 0) < iota((total, total), 1)
    )
    before = matmul(named.astype(jnp.float32).astype(jnp.bfloat16), earlier.astype(jnp.float32).astype(jnp.bfloat16))
    column = iota((8, total), 1)
    first = column // tokens * slots + column // rows % 2 * CAP
    place = jnp.where(named, first + before.astype(jnp.int32), -1)
    for apart in range(EXPERTS):
        hit = iota((PARTS * slots, total), 0) == place[apart:apart + 1, :]
        outs[apart][...] = matmul(hit.astype(jnp.float32).astype(jnp.bfloat16), stacked[...]).astype(jnp.bfloat16)


def pack(me, state, route, rows):
    tokens, half = state.shape
    shape = (PARTS * 2 * CAP, half // PARTS)
    return pl.pallas_call(
        functools.partial(pack_kernel, rows),
        out_shape=[jax.ShapeDtypeStruct(shape, jnp.bfloat16)] * EXPERTS,
        in_specs=[pl.BlockSpec(memory_space=pltpu.SMEM)] + [pl.BlockSpec(memory_space=pltpu.VMEM)] * 2,
        out_specs=[pl.BlockSpec(memory_space=pltpu.VMEM)] * EXPERTS,
        scratch_shapes=[pltpu.VMEM((PARTS * tokens, half // PARTS), jnp.bfloat16)],
        compiler_params=params(),
        name="pack",
    )(me, state, route)


def first_kernel(me, r0, r1, r2, r3, gain, weight, partial, rows_out, squares, stacked):
    slots = 2 * CAP
    block = PARTS * slots
    width = r0.shape[1]

    @pl.when(pl.program_id(0) == 0)
    def _():
        for apart, ref in enumerate((r0, r1, r2, r3)):
            stacked[apart * block:(apart + 1) * block, :] = ref[...]
        row = iota((block, EXPERTS * block), 0)
        column = iota((block, EXPERTS * block), 1)
        total = jnp.zeros((block, 1), jnp.float32)
        for part in range(PARTS):
            source = row // slots * block + part * slots + row % slots
            pick = (column == source).astype(jnp.float32).astype(jnp.bfloat16)
            values = matmul(pick, stacked[...])
            total = total + jnp.sum(values * values, axis=1, keepdims=True)
            scaled = values * gain[part:part + 1, :]
            rows_out[:, part * width:(part + 1) * width] = scaled.astype(jnp.bfloat16)
        squares[...] = jnp.broadcast_to(total, squares.shape)

    partial[...] = matmul(rows_out[...], weight[...]).astype(partial.dtype)


def column_block(step, side, count, blocks):
    return step // blocks * count + side * blocks + step % blocks


def first(me, received, gain, weight, step_width=256):
    block, width = received[0].shape
    half = PARTS * width
    both = weight.shape[1]
    blocks = both // 4 // step_width
    whole = pl.BlockSpec(memory_space=pltpu.VMEM)
    fixed = lambda shape: pl.BlockSpec(shape, lambda step, me: (0, 0))
    return pl.pallas_call(
        first_kernel,
        out_shape=[
            jax.ShapeDtypeStruct((block, both // 2), jnp.bfloat16),
            jax.ShapeDtypeStruct((block, half), jnp.bfloat16),
            jax.ShapeDtypeStruct((block, 128), jnp.float32),
        ],
        grid_spec=pltpu.PrefetchScalarGridSpec(
            num_scalar_prefetch=1,
            grid=(2 * blocks,),
            in_specs=[fixed((block, width))] * EXPERTS + [
                fixed((PARTS, width)),
                pl.BlockSpec(
                    (half, step_width),
                    lambda step, me: (0, column_block(step, 1 - me[1], 2 * blocks, blocks)),
                ),
            ],
            out_specs=[
                pl.BlockSpec((block, step_width), lambda step, me: (0, step)),
                fixed((block, half)),
                fixed((block, 128)),
            ],
            scratch_shapes=[pltpu.VMEM((EXPERTS * block, width), jnp.bfloat16)],
        ),
        compiler_params=params(),
        cost_estimate=pl.CostEstimate(flops=2 * block * half * both // 2, bytes_accessed=half * both, transcendentals=0),
        name="first",
    )(me, *received, gain, weight)


def second_kernel(me, rows_in, weight, partial):
    partial[...] = matmul(rows_in[...], weight[...])


def second(me, rows_in, weight, step_width=256):
    block, half = rows_in.shape
    both = weight.shape[1]
    blocks = both // 4 // step_width
    return pl.pallas_call(
        second_kernel,
        out_shape=jax.ShapeDtypeStruct((block, both // 2), jnp.float32),
        grid_spec=pltpu.PrefetchScalarGridSpec(
            num_scalar_prefetch=1,
            grid=(2 * blocks,),
            in_specs=[
                pl.BlockSpec((block, half), lambda step, me: (0, 0)),
                pl.BlockSpec(
                    (half, step_width),
                    lambda step, me: (0, column_block(step, me[1], 2 * blocks, blocks)),
                ),
            ],
            out_specs=pl.BlockSpec((block, step_width), lambda step, me: (0, step)),
        ),
        compiler_params=params(),
        cost_estimate=pl.CostEstimate(flops=2 * block * half * both // 2, bytes_accessed=half * both, transcendentals=0),
        name="second",
    )(me, rows_in, weight)


def act_kernel(model_width, own, other, squares, squares_other, hidden):
    units = hidden.shape[1]
    mean = (squares[:, 0:1] + squares_other[:, 0:1]) / model_width
    scale = lax.rsqrt(mean + EPSILON)
    summed = (own[...] + other[...].astype(jnp.float32)) * scale
    gate = summed[:, :units]
    hidden[...] = (gate / (1.0 + jnp.exp(-gate)) * summed[:, units:]).astype(jnp.bfloat16)


def act(own, other, squares, squares_other, model_width):
    block, both = own.shape
    return pl.pallas_call(
        functools.partial(act_kernel, model_width),
        out_shape=jax.ShapeDtypeStruct((block, both // 2), jnp.bfloat16),
        in_specs=[pl.BlockSpec(memory_space=pltpu.VMEM)] * 4,
        out_specs=pl.BlockSpec(memory_space=pltpu.VMEM),
        compiler_params=params(),
        name="act",
    )(own, other, squares, squares_other)


def third_kernel(me, hidden, weight, partial):
    partial[...] = matmul(hidden[...], weight[...])


def third(me, hidden, weight):
    block, units = hidden.shape
    half = weight.shape[1]
    width = half // PARTS
    return pl.pallas_call(
        third_kernel,
        out_shape=jax.ShapeDtypeStruct((block, half), jnp.float32),
        grid_spec=pltpu.PrefetchScalarGridSpec(
            num_scalar_prefetch=1,
            grid=(PARTS,),
            in_specs=[
                pl.BlockSpec((block, units), lambda step, me: (0, 0)),
                pl.BlockSpec((units, width), lambda step, me: (me[1], step)),
            ],
            out_specs=pl.BlockSpec((block, width), lambda step, me: (0, step)),
        ),
        compiler_params=params(),
        cost_estimate=pl.CostEstimate(flops=2 * block * half * units, bytes_accessed=2 * half * units, transcendentals=0),
        name="third",
    )(me, hidden, weight)


def fourth_kernel(me, hidden, weight, own, o0, o1, o2, o3, stacked):
    slots = 2 * CAP
    block = PARTS * slots
    step = pl.program_id(0)
    result = own[...] + matmul(hidden[...], weight[...])
    start = pl.multiple_of(step * block, block)
    stacked[pl.ds(start, block), :] = result.astype(jnp.bfloat16)

    @pl.when(step == PARTS - 1)
    def _():
        row = iota((block, EXPERTS * block), 0)
        column = iota((block, EXPERTS * block), 1)
        for apart, out in enumerate((o0, o1, o2, o3)):
            source = row // slots * block + apart * slots + row % slots
            pick = (column == source).astype(jnp.float32).astype(jnp.bfloat16)
            out[...] = matmul(pick, stacked[...]).astype(jnp.bfloat16)


def fourth(me, hidden, weight, own):
    block, units = hidden.shape
    half = weight.shape[1]
    width = half // PARTS
    return pl.pallas_call(
        fourth_kernel,
        out_shape=[jax.ShapeDtypeStruct((block, width), jnp.bfloat16)] * EXPERTS,
        grid_spec=pltpu.PrefetchScalarGridSpec(
            num_scalar_prefetch=1,
            grid=(PARTS,),
            in_specs=[
                pl.BlockSpec((block, units), lambda step, me: (0, 0)),
                pl.BlockSpec((units, width), lambda step, me: (1 - me[1], step)),
                pl.BlockSpec((block, width), lambda step, me: (0, step)),
            ],
            out_specs=[pl.BlockSpec((block, width), lambda step, me: (0, 0))] * EXPERTS,
            scratch_shapes=[pltpu.VMEM((PARTS * block, width), jnp.bfloat16)],
        ),
        compiler_params=params(),
        cost_estimate=pl.CostEstimate(flops=2 * block * half * units, bytes_accessed=2 * half * units, transcendentals=0),
        name="fourth",
    )(me, hidden, weight, own)


def mix_kernel(rows, me, state, route, share, r0, r1, r2, r3, out):
    tokens, half = state.shape
    width = half // PARTS
    total = PARTS * tokens
    slots = 2 * CAP
    expert = me[0] ^ iota((total, 128), 1)
    named = (route[:, 0:1] == expert) | (route[:, 1:2] == expert)
    weight = jnp.where(route[:, 0:1] == expert, share[:, 0:1], 0.0) + jnp.where(
        route[:, 1:2] == expert, share[:, 1:2], 0.0
    )
    earlier = (iota((total, total), 0) // rows == iota((total, total), 1) // rows) & (
        iota((total, total), 0) > iota((total, total), 1)
    )
    before = matmul(earlier.astype(jnp.float32).astype(jnp.bfloat16), named.astype(jnp.float32).astype(jnp.bfloat16))
    line = iota((total, 128), 0)
    first = line // tokens * slots + line // rows % 2 * CAP
    place = jnp.where(named, first + before.astype(jnp.int32), -1)
    mixed = jnp.zeros((total, width), jnp.float32)
    for apart, ref in enumerate((r0, r1, r2, r3)):
        hit = iota((total, PARTS * slots), 1) == place[:, apart:apart + 1]
        spread = jnp.where(hit, weight[:, apart:apart + 1], 0.0)
        high = spread.astype(jnp.bfloat16)
        low = (spread - high.astype(jnp.float32)).astype(jnp.bfloat16)
        mixed = mixed + matmul(high, ref[...]) + matmul(low, ref[...])
    for part in range(PARTS):
        span = slice(part * width, (part + 1) * width)
        summed = state[:, span].astype(jnp.float32) + mixed[part * tokens:(part + 1) * tokens, :]
        out[:, span] = summed.astype(jnp.bfloat16)


def mix(me, state, route, share, received, rows):
    return pl.pallas_call(
        functools.partial(mix_kernel, rows),
        out_shape=jax.ShapeDtypeStruct(state.shape, jnp.bfloat16),
        in_specs=[pl.BlockSpec(memory_space=pltpu.SMEM)] + [pl.BlockSpec(memory_space=pltpu.VMEM)] * 7,
        out_specs=pl.BlockSpec(memory_space=pltpu.VMEM),
        compiler_params=params(),
        name="mix",
    )(me, state, route, share, *received)


def across(blocks):
    size = lax.axis_size("expert")
    moved = [blocks[0]]
    for apart in range(1, EXPERTS):
        moved.append(lax.ppermute(blocks[apart], "expert", [(i, i ^ 2 * apart) for i in range(size)]))
    return moved


def gathered_pair(block, x, axis):
    other = partner(block, "expert", 0)
    return jnp.concatenate([jnp.where(x == 0, block, other), jnp.where(x == 0, other, block)], axis=axis)


def to_halves(batch, x):
    half = batch.shape[1] // 2
    kept = lax.dynamic_slice_in_dim(batch, x * half, half, 1)
    sent = lax.dynamic_slice_in_dim(batch, (1 - x) * half, half, 1)
    other = partner(sent, "expert", 0)
    return jnp.concatenate([jnp.where(x == 0, kept, other), jnp.where(x == 0, other, kept)], axis=0)


def to_rows(state, x):
    rows = state.shape[0] // 2
    kept = lax.dynamic_slice_in_dim(state, x * rows, rows, 0)
    sent = lax.dynamic_slice_in_dim(state, (1 - x) * rows, rows, 0)
    other = partner(sent, "expert", 0)
    return jnp.concatenate([jnp.where(x == 0, kept, other), jnp.where(x == 0, other, kept)], axis=1)


def paired_shards(
    east_batch,
    west_batch,
    east_entering,
    west_entering,
    east_experts,
    west_experts,
    east_gates,
    west_gates,
    norm_gain,
    expert_in,
    expert_down,
):
    section_index = lax.axis_index("pipe")
    section_count = lax.axis_size("pipe")
    member = lax.axis_index("expert")
    x = member % 2
    me = jnp.stack([member // 2, x]).astype(jnp.int32)
    rows, model_width = east_batch.shape[1:]
    half = model_width // 2
    weight_in = expert_in[0, 0]
    weight_out = expert_down[0, 0]
    gain = lax.dynamic_slice_in_dim(norm_gain[0], x * half, half, 0).reshape(PARTS, half // PARTS)

    table = jnp.stack([east_experts[:, 0], west_experts[:, 0]]).astype(jnp.float32)
    table = jnp.concatenate([table, jnp.stack([east_gates[:, 0], west_gates[:, 0]])], axis=3)
    table = gathered_pair(table, x, 2)
    table = jnp.tile(table, (1, 1, PARTS, 1))
    routes = table[..., :2].astype(jnp.int32)
    routes_row = jnp.swapaxes(routes, 2, 3)
    shares = table[..., 2:]

    now = [to_halves(east_batch[0], x), to_halves(west_batch[0], x)]
    entering = [to_halves(east_entering[0], x), to_halves(west_entering[0], x)]
    for tick in range(TICKS):
        for stream in range(2):
            state = now[stream]
            received = across(pack(me, state, routes_row[stream, tick], rows))
            sent, scaled, squares = first(me, received, gain, weight_in)
            other = partner(sent, "expert", 0)
            squares_other = partner(squares, "expert", 0)
            own = second(me, scaled, weight_in)
            hidden = act(own, other, squares, squares_other, model_width)
            hidden_other = partner(hidden, "expert", 0)
            result = third(me, hidden, weight_out)
            returned = across(fourth(me, hidden_other, weight_out, result))
            state = mix(me, state, routes[stream, tick], shares[stream, tick], returned, rows)
            if tick + 1 < TICKS:
                step = 1 - 2 * stream
                edge = 0 if stream == 0 else section_count - 1
                state = jnp.where(section_index == edge, entering[stream], shifted(state, "pipe", step))
            now[stream] = state
    return (to_rows(now[0], x)[None], to_rows(now[1], x)[None])


def solution(mesh):
    in_specs = (
        P("pipe", "expert", None),
        P("pipe", "expert", None),
        P(None, "expert", None),
        P(None, "expert", None),
        P(None, "pipe", "expert", None),
        P(None, "pipe", "expert", None),
        P(None, "pipe", "expert", None),
        P(None, "pipe", "expert", None),
        P("pipe", None),
        P("pipe", "expert", None, None),
        P("pipe", "expert", None, None),
    )
    out_specs = (P("pipe", "expert", None), P("pipe", "expert", None))
    groups = mesh.shape["expert"] // EXPERTS
    shards = paired_shards if groups == 2 else general_shards
    return jax.shard_map(shards, mesh=mesh, in_specs=in_specs, out_specs=out_specs, check_vma=False)
```

```python
import functools

import jax
import jax.numpy as jnp
from jax import lax
from jax.experimental import pallas as pl
from jax.experimental.pallas import tpu as pltpu
from jax.sharding import PartitionSpec as P

EXPERTS = 4
TICKS = 2
CAP = 18


EPSILON = 1e-06


def partner(shard, axis, apart):
    return lax.ppermute(shard, axis, [(i, i ^ 1 << apart) for i in range(lax.axis_size(axis))])


def shifted(block, axis, distance):
    devices = range(lax.axis_size(axis))
    route = [(i - distance, i) for i in devices if i - distance in devices]
    return lax.ppermute(block, axis, route)


def rms_scaled(joined_rows, gain_row):
    values = joined_rows.astype(jnp.float32)
    scale_row = lax.rsqrt(jnp.mean(values * values, axis=-1, keepdims=True) + EPSILON)
    return (values * scale_row * gain_row[None, :]).astype(jnp.bfloat16)


def slot_tables(joined_routes, joined_shares, batch_count, experts, capacity):
    total_rows = joined_routes.shape[0]
    row_count = total_rows // batch_count
    onehot = (
        joined_routes[:, :, None] == jnp.arange(experts, dtype=jnp.int32)[None, None, :]
    ).astype(jnp.int32)
    per_row = jnp.sum(onehot, axis=1).reshape(batch_count, row_count, experts)
    before = (jnp.cumsum(per_row, axis=1) - per_row).reshape(total_rows, experts)
    slot_of = jnp.sum(onehot * before[:, None, :], axis=2)
    offset = jnp.arange(total_rows, dtype=jnp.int32) // row_count * capacity
    slot_of = slot_of + offset[:, None]
    slot_ids = jnp.arange(batch_count * capacity, dtype=jnp.int32)
    slot_hit = (slot_of[:, :, None] == slot_ids[None, None, :]).astype(jnp.float32)
    onehot_float = onehot.astype(jnp.float32)
    placement = jnp.einsum("rke,rkc->ecr", onehot_float, slot_hit, precision=lax.Precision.HIGHEST)
    weighted = jnp.einsum(
        "rke,rkc->rec",
        onehot_float * joined_shares[:, :, None],
        slot_hit,
        precision=lax.Precision.HIGHEST,
    )
    return (placement, weighted)


def halving_sum(partial_value, groups, halved_bits):
    row_count = partial_value.shape[0]
    slice_width = partial_value.shape[1] // (2 * groups)
    holding = partial_value.reshape(row_count, 2, groups, slice_width)
    member_index = lax.axis_index("expert")
    held_count = groups
    for bit_index in range(halved_bits):
        own_bit = member_index >> bit_index & 1
        reshaped = holding.reshape(row_count, 2, held_count // 2, 2, slice_width)
        kept_half = lax.dynamic_index_in_dim(reshaped, own_bit, 3, keepdims=False)
        sent_half = lax.dynamic_index_in_dim(reshaped, 1 - own_bit, 3, keepdims=False)
        holding = kept_half + partner(sent_half, "expert", bit_index)
        held_count = held_count // 2
    holding = holding + partner(holding, "expert", halved_bits)
    return (holding[:, 0], holding[:, 1])


def doubling_gather(own_piece, gathered_bits):
    row_count, held_count, slice_width = own_piece.shape
    holding = own_piece
    member_index = lax.axis_index("expert")
    for bit_index in reversed(range(gathered_bits)):
        own_bit = member_index >> bit_index & 1
        arrived = partner(holding, "expert", bit_index)
        first_half = jnp.where(own_bit == 0, holding, arrived)
        second_half = jnp.where(own_bit == 0, arrived, holding)
        stacked = jnp.stack([first_half, second_half], axis=2)
        holding = stacked.reshape(row_count, -1, slice_width)
    return holding.reshape(row_count, -1)


def expert_layer(batch_list, route_list, share_list, gain_row, weight_in, weight_out):
    batch_count = len(batch_list)
    row_count = batch_list[0].shape[0]
    model_width = batch_list[0].shape[1]
    groups = lax.axis_size("expert") // EXPERTS
    bit_count = groups.bit_length() - 1
    halved_bits = bit_count - 1
    feat_width = model_width // groups
    joined_rows = batch_list[0]
    joined_routes = route_list[0]
    joined_shares = share_list[0]
    normed = rms_scaled(joined_rows, gain_row)
    placement, weighted = slot_tables(joined_routes, joined_shares, batch_count, EXPERTS, CAP)
    total_rows = batch_count * row_count
    normed_split = normed.reshape(total_rows, groups, feat_width)
    outgoing = jnp.einsum(
        "ecr,rwf->ewcf",
        placement.astype(jnp.bfloat16),
        normed_split,
        preferred_element_type=jnp.float32,
    ).astype(jnp.bfloat16)
    outgoing = outgoing.reshape(EXPERTS * groups, batch_count * CAP, feat_width)
    arrived = lax.all_to_all(outgoing, "expert", split_axis=0, concat_axis=0, tiled=True)
    sources, slot_count, block_width = arrived.shape
    flat_rows = arrived.reshape(sources * slot_count, block_width)
    partial_value = jnp.dot(flat_rows, weight_in, preferred_element_type=jnp.float32)
    gate_part, up_part = halving_sum(partial_value, groups, halved_bits)
    own_piece = (jax.nn.silu(gate_part) * up_part).astype(jnp.bfloat16)
    hidden = doubling_gather(own_piece, halved_bits)
    result = jnp.dot(hidden, weight_out, preferred_element_type=jnp.float32).astype(jnp.bfloat16)
    returned = lax.all_to_all(
        result.reshape(sources, slot_count, block_width),
        "expert",
        split_axis=0,
        concat_axis=0,
        tiled=True,
    )
    returned_split = returned.reshape(EXPERTS, groups, batch_count * CAP, feat_width).astype(
        jnp.float32
    )
    mixed = jnp.einsum(
        "rec,ewcf->rwf", weighted, returned_split, precision=lax.Precision.HIGHEST
    ).reshape(total_rows, model_width)
    output = (joined_rows.astype(jnp.float32) + mixed).astype(jnp.bfloat16)
    return [output]


def general_shards(
    east_batch,
    west_batch,
    east_entering,
    west_entering,
    east_experts,
    west_experts,
    east_gates,
    west_gates,
    norm_gain,
    expert_in,
    expert_down,
):
    section_index = lax.axis_index("pipe")
    section_count = lax.axis_size("pipe")
    gain_row = norm_gain[0]
    weight_in = expert_in[0, 0]
    weight_out = expert_down[0, 0]
    east_now = east_batch[0]
    west_now = west_batch[0]
    for tick_index in range(TICKS):
        east_routes = east_experts[tick_index, 0]
        west_routes = west_experts[tick_index, 0]
        east_shares = east_gates[tick_index, 0]
        west_shares = west_gates[tick_index, 0]
        east_now = expert_layer(
            [east_now], [east_routes], [east_shares], gain_row, weight_in, weight_out
        )[0]
        west_now = expert_layer(
            [west_now], [west_routes], [west_shares], gain_row, weight_in, weight_out
        )[0]
        if tick_index + 1 < TICKS:
            moved_east = shifted(east_now, "pipe", 1)
            east_now = jnp.where(section_index == 0, east_entering[tick_index], moved_east)
            moved_west = shifted(west_now, "pipe", -1)
            west_now = jnp.where(
                section_index == section_count - 1, west_entering[tick_index], moved_west
            )
    return (east_now[None], west_now[None])


PARTS = 4
LIMIT = 16 * 2**20


def whole(count):
    return [pl.BlockSpec(memory_space=pltpu.VMEM)] * count


def without(kernel, place, count, *refs):
    kernel(*refs[:place], *refs[place + count:])


def call(kernel, name, out_shape, me, *arrays, after=(), scratch=(), flops=0, limit=LIMIT):
    several = isinstance(out_shape, list)
    if after:
        kernel = functools.partial(without, kernel, 1 + len(arrays), len(after))
    unread = [pl.BlockSpec(memory_space=pl.ANY)] * len(after)
    return pl.pallas_call(
        kernel,
        out_shape=out_shape,
        in_specs=[pl.BlockSpec(memory_space=pltpu.SMEM)] + whole(len(arrays)) + unread,
        out_specs=whole(len(out_shape)) if several else whole(1)[0],
        scratch_shapes=list(scratch),
        compiler_params=pltpu.CompilerParams(vmem_limit_bytes=limit),
        cost_estimate=pl.CostEstimate(flops=flops, bytes_accessed=0, transcendentals=0),
        name=name,
    )(me, *arrays, *after)


def bf16(*shape):
    return jax.ShapeDtypeStruct(shape, jnp.bfloat16)


def f32(*shape):
    return jax.ShapeDtypeStruct(shape, jnp.float32)


def iota(shape, axis):
    return lax.broadcasted_iota(jnp.int32, shape, axis)


def matmul(a, b):
    return jnp.dot(a, b, preferred_element_type=jnp.float32)


def ones_where(condition):
    return condition.astype(jnp.float32).astype(jnp.bfloat16)


def pieces(values):
    high = values.astype(jnp.bfloat16)
    rest = values - high.astype(jnp.float32)
    middle = rest.astype(jnp.bfloat16)
    return high, middle, (rest - middle.astype(jnp.float32)).astype(jnp.bfloat16)


def cut_kernel(me, batch, sent):
    half = sent.shape[1]
    sent[...] = batch[:, pl.ds(pl.multiple_of((1 - me[1]) * half, half), half)]


def cut(me, batch):
    rows, model_width = batch.shape
    return call(cut_kernel, "cut", bf16(rows, model_width // 2), me, batch)


def tables_kernel(me, own, other, as_rows, as_columns):
    rows = own.shape[1]
    total = as_rows.shape[1]
    row_sum = jnp.zeros(as_rows.shape, jnp.float32)
    column_sum = jnp.zeros(as_columns.shape, jnp.float32)
    for source, x in ((own, me[1]), (other, 1 - me[1])):
        token, column = iota((rows, total), 0), iota((rows, total), 1)
        spread = ones_where((column % rows == token) & (column // rows % 2 == x))
        line, lane = iota((total, rows), 0), iota((total, rows), 1)
        gather = ones_where((line % rows == lane) & (line // rows % 2 == x))
        high, middle, low = pieces(source[...])
        row_sum = row_sum + ((matmul(low, spread) + matmul(middle, spread)) + matmul(high, spread))
        turned = [
            lax.dot_general(gather, piece, (((1,), (1,)), ((), ())), preferred_element_type=jnp.float32)
            for piece in (low, middle, high)
        ]
        column_sum = column_sum + ((turned[0] + turned[1]) + turned[2])
    as_rows[...] = row_sum
    as_columns[...] = column_sum


def tables(me, own, other):
    kinds, rows = own.shape
    total = 2 * PARTS * rows
    return call(tables_kernel, "tables", [f32(kinds, total), f32(total, kinds)], me, own, other)


def joined(me, batch, other, state):
    rows, half = other.shape
    kept = batch[:, pl.ds(pl.multiple_of(me[1] * half, half), half)]
    state[pl.ds(pl.multiple_of(me[1] * rows, rows), rows), :] = kept
    state[pl.ds(pl.multiple_of((1 - me[1]) * rows, rows), rows), :] = other[...]


def packed(me, state, table, turn, outs, stacked):
    tokens, half = state.shape
    rows = tokens // 2
    width = half // PARTS
    total = PARTS * tokens
    slots = 2 * CAP
    for part in range(PARTS):
        stacked[part * tokens:(part + 1) * tokens, :] = state[:, part * width:(part + 1) * width]
    expert = me[0] ^ iota((8, total), 0)
    chosen = table[4 * turn:4 * turn + 2, :].astype(jnp.int32)
    named = (chosen[0:1, :] == expert) | (chosen[1:2, :] == expert)
    earlier = (iota((total, total), 0) // rows == iota((total, total), 1) // rows) & (
        iota((total, total), 0) < iota((total, total), 1)
    )
    before = matmul(ones_where(named), ones_where(earlier))
    column = iota((8, total), 1)
    start = column // tokens * slots + column // rows % 2 * CAP
    place = jnp.where(named, start + before.astype(jnp.int32), -1)
    for apart in range(EXPERTS):
        hit = iota((PARTS * slots, total), 0) == place[apart:apart + 1, :]
        outs[apart][...] = matmul(ones_where(hit), stacked[...]).astype(jnp.bfloat16)


def enter_kernel(turn, me, batch, other, table, o0, o1, o2, o3, state, stacked):
    joined(me, batch, other, state)
    packed(me, state, table, turn, (o0, o1, o2, o3), stacked)


def relay_kernel(turn, edge, me, moved, batch, other, table, o0, o1, o2, o3, state, stacked):
    state[...] = moved[...]

    @pl.when(me[2 + edge] == 1)
    def _():
        joined(me, batch, other, state)

    packed(me, state, table, turn, (o0, o1, o2, o3), stacked)


def pack_shapes(rows, half):
    width = half // PARTS
    outs = [bf16(PARTS * 2 * CAP, width)] * EXPERTS + [bf16(2 * rows, half)]
    return outs, [pltpu.VMEM((PARTS * 2 * rows, width), jnp.bfloat16)]


def enter(me, turn, batch, other, table):
    outs, scratch = pack_shapes(*other.shape)
    made = call(functools.partial(enter_kernel, turn), "enter", outs, me, batch, other, table, scratch=scratch)
    return made[:EXPERTS], made[EXPERTS]


def relay(me, turn, edge, moved, batch, other, table):
    outs, scratch = pack_shapes(*other.shape)
    kernel = functools.partial(relay_kernel, turn, edge)
    made = call(kernel, "relay", outs, me, moved, batch, other, table, scratch=scratch)
    return made[:EXPERTS], made[EXPERTS]


def first_kernel(me, r0, r1, r2, r3, gain, weight, partial, rows_out, squares, stacked):
    slots = 2 * CAP
    block = PARTS * slots
    width = r0.shape[1]
    units = weight.shape[1] // 4
    for apart, ref in enumerate((r0, r1, r2, r3)):
        stacked[apart * block:(apart + 1) * block, :] = ref[...]
    row = iota((block, EXPERTS * block), 0)
    column = iota((block, EXPERTS * block), 1)
    total = jnp.zeros((block, 1), jnp.float32)
    for part in range(PARTS):
        source = row // slots * block + part * slots + row % slots
        pick = (column == source).astype(jnp.float32).astype(jnp.bfloat16)
        values = matmul(pick, stacked[...])
        total = total + jnp.sum(values * values, axis=1, keepdims=True)
        start = pl.multiple_of(me[1] * PARTS * width + part * width, width)
        scaled = values * gain[:, pl.ds(start, width)]
        rows_out[:, part * width:(part + 1) * width] = scaled.astype(jnp.bfloat16)
    squares[...] = jnp.broadcast_to(total, squares.shape)
    lane = iota(squares.shape, 1)
    high, middle, low = [piece.astype(jnp.float32) for piece in pieces(total)]
    sent = jnp.where(lane == 0, high, jnp.where(lane == 1, middle, jnp.where(lane == 2, low, 0.0)))
    partial[:, 2 * units:] = sent.astype(jnp.bfloat16)
    for kind in range(2):
        start = pl.multiple_of(2 * units * kind + units * (1 - me[1]), units)
        columns = matmul(rows_out[...], weight[:, pl.ds(start, units)])
        partial[:, kind * units:(kind + 1) * units] = columns.astype(jnp.bfloat16)


def first(me, received, gain, weight, after):
    block, width = received[0].shape
    half, both = weight.shape
    outs = [bf16(block, both // 2 + 128), bf16(block, half), f32(block, 128)]
    scratch = [pltpu.VMEM((EXPERTS * block, width), jnp.bfloat16)]
    return call(first_kernel, "first", outs, me, *received, gain, weight, after=after, scratch=scratch, flops=block * half * both)


def second_kernel(me, rows_in, weight, own):
    units = weight.shape[1] // 4
    for kind in range(2):
        start = pl.multiple_of(2 * units * kind + units * me[1], units)
        own[:, kind * units:(kind + 1) * units] = matmul(rows_in[...], weight[:, pl.ds(start, units)])


def second(me, rows_in, weight):
    block, half = rows_in.shape
    both = weight.shape[1]
    return call(second_kernel, "second", f32(block, both // 2), me, rows_in, weight, flops=block * half * both)


def act_kernel(model_width, me, own, other, squares, hidden):
    units = hidden.shape[1]
    arrived = other[:, 2 * units:].astype(jnp.float32)
    mean = (squares[:, 0:1] + ((arrived[:, 2:3] + arrived[:, 1:2]) + arrived[:, 0:1])) / model_width
    scale = lax.rsqrt(mean + EPSILON)
    gate = (own[:, :units] + other[:, :units].astype(jnp.float32)) * scale
    up = (own[:, units:] + other[:, units:2 * units].astype(jnp.float32)) * scale
    hidden[...] = (gate / (1.0 + jnp.exp(-gate)) * up).astype(jnp.bfloat16)


def act(me, own, other, squares, model_width):
    block, both = own.shape
    return call(functools.partial(act_kernel, model_width), "act", bf16(block, both // 2), me, own, other, squares)


def third_kernel(me, hidden, hidden_other, weight, o0, o1, o2, o3, stacked):
    slots = 2 * CAP
    block, units = hidden.shape
    width = o0.shape[1]
    own_rows = pl.ds(pl.multiple_of(units * me[1], units), units)
    other_rows = pl.ds(pl.multiple_of(units * (1 - me[1]), units), units)
    for part in range(PARTS):
        columns = slice(part * width, (part + 1) * width)
        result = matmul(hidden[...], weight[own_rows, columns]) + matmul(hidden_other[...], weight[other_rows, columns])
        stacked[part * block:(part + 1) * block, :] = result.astype(jnp.bfloat16)
    row = iota((block, PARTS * block), 0)
    column = iota((block, PARTS * block), 1)
    for apart, out in enumerate((o0, o1, o2, o3)):
        source = row // slots * block + apart * slots + row % slots
        pick = (column == source).astype(jnp.float32).astype(jnp.bfloat16)
        out[...] = matmul(pick, stacked[...]).astype(jnp.bfloat16)


def third(me, hidden, hidden_other, weight):
    block, units = hidden.shape
    half = weight.shape[1]
    width = half // PARTS
    outs = [bf16(block, width)] * EXPERTS
    scratch = [pltpu.VMEM((PARTS * block, width), jnp.bfloat16)]
    flops = 4 * block * half * units
    return call(third_kernel, "third", outs, me, hidden, hidden_other, weight, scratch=scratch, flops=flops)


def mixed_parts(me, table, turn, received, tokens):
    rows = tokens // 2
    width = received[0].shape[1]
    total = PARTS * tokens
    slots = 2 * CAP
    expert = me[0] ^ iota((total, 128), 1)
    chosen = table[:, 4 * turn:4 * turn + 2].astype(jnp.int32)
    share = table[:, 4 * turn + 2:4 * turn + 4]
    hits = [chosen[:, k:k + 1] == expert for k in range(2)]
    weight = jnp.where(hits[0], share[:, 0:1], 0.0) + jnp.where(hits[1], share[:, 1:2], 0.0)
    named = hits[0] | hits[1]
    earlier = (iota((total, total), 0) // rows == iota((total, total), 1) // rows) & (
        iota((total, total), 0) > iota((total, total), 1)
    )
    before = matmul(ones_where(earlier), ones_where(named))
    line = iota((total, 128), 0)
    start = line // tokens * slots + line // rows % 2 * CAP
    place = jnp.where(named, start + before.astype(jnp.int32), -1)
    mixed = jnp.zeros((total, width), jnp.float32)
    for apart, ref in enumerate(received):
        hit = iota((total, PARTS * slots), 1) == place[:, apart:apart + 1]
        spread = jnp.where(hit, weight[:, apart:apart + 1], 0.0)
        high = spread.astype(jnp.bfloat16)
        low = (spread - high.astype(jnp.float32)).astype(jnp.bfloat16)
        mixed = mixed + matmul(high, ref[...]) + matmul(low, ref[...])
    return mixed


def mix_kernel(turn, me, state, table, r0, r1, r2, r3, out):
    tokens = state.shape[0]
    width = r0.shape[1]
    mixed = mixed_parts(me, table, turn, (r0, r1, r2, r3), tokens)
    for part in range(PARTS):
        span = slice(part * width, (part + 1) * width)
        summed = state[:, span].astype(jnp.float32) + mixed[part * tokens:(part + 1) * tokens, :]
        out[:, span] = summed.astype(jnp.bfloat16)


def mix(me, turn, state, table, received, after):
    kernel = functools.partial(mix_kernel, turn)
    return call(kernel, "mix", bf16(*state.shape), me, state, table, *received, after=after)


def last_kernel(turn, me, state, table, r0, r1, r2, r3, kept, sent, result):
    rows = kept.shape[0]
    mix_kernel(turn, me, state, table, r0, r1, r2, r3, result)
    kept[...] = result[pl.ds(pl.multiple_of(me[1] * rows, rows), rows), :]
    sent[...] = result[pl.ds(pl.multiple_of((1 - me[1]) * rows, rows), rows), :]


def last(me, turn, state, table, received, after):
    tokens, half = state.shape
    outs = [bf16(tokens // 2, half)] * 2
    scratch = [pltpu.VMEM(state.shape, jnp.bfloat16)]
    return call(functools.partial(last_kernel, turn), "last", outs, me, state, table, *received, after=after, scratch=scratch)


def finish_kernel(me, kept, other, out):
    half = kept.shape[1]
    out[:, pl.ds(pl.multiple_of(me[1] * half, half), half)] = kept[...]
    out[:, pl.ds(pl.multiple_of((1 - me[1]) * half, half), half)] = other[...]


def finish(me, kept, other):
    return call(finish_kernel, "finish", bf16(kept.shape[0], 2 * kept.shape[1]), me, kept, other)


def across(blocks, behind=None):
    size = lax.axis_size("expert")
    blocks = list(blocks)
    if behind is not None:
        *blocks, behind[2] = lax.optimization_barrier((*blocks, behind[2]))
    moved = list(blocks)
    for apart in (2, 3, 1):
        moved[apart] = lax.ppermute(blocks[apart], "expert", [(i, i ^ 2 * apart) for i in range(size)])
    return moved


def paired_shards(
    east_batch,
    west_batch,
    east_entering,
    west_entering,
    east_experts,
    west_experts,
    east_gates,
    west_gates,
    norm_gain,
    expert_in,
    expert_down,
):
    section_index = lax.axis_index("pipe")
    section_count = lax.axis_size("pipe")
    member = lax.axis_index("expert")
    edges = [section_index == 0, section_index == section_count - 1]
    me = jnp.stack([member // 2, member % 2, *edges]).astype(jnp.int32)
    rows, model_width = east_batch.shape[1:]
    weight_in = expert_in[0, 0]
    weight_out = expert_down[0, 0]
    kinds = [
        jnp.swapaxes(array[tick, 0], 0, 1).astype(jnp.float32)
        for experts, gates in ((east_experts, east_gates), (west_experts, west_gates))
        for tick in range(TICKS)
        for array in (experts, gates)
    ]
    lists = jnp.concatenate(kinds, axis=0)

    batches = [east_batch[0], west_batch[0]]
    entering = [east_entering[0], west_entering[0]]
    batches_other = [partner(cut(me, batch), "expert", 0) for batch in batches]
    as_rows, as_columns = tables(me, lists, partner(lists, "expert", 0))
    entering_other = [partner(cut(me, batch), "expert", 0) for batch in entering]
    moved = [None, None]
    results = [None, None]
    states = [None, None]
    ahead = None
    for tick in range(TICKS):
        final = tick + 1 == TICKS
        arrived = [None, None]
        for stream in range(2):
            turn = stream * TICKS + tick
            if tick == 0:
                sent, states[stream] = enter(me, turn, batches[stream], batches_other[stream], as_rows)
            else:
                sent, states[stream] = relay(
                    me, turn, stream, moved[stream], entering[stream], entering_other[stream], as_rows
                )
                if stream == 0:
                    moved[1] = shifted(mix(me, turn_before, state_before, as_columns, ahead, [sent[0]]), "pipe", -1)
            arrived[stream] = across(sent, ahead)
            ahead = arrived[stream]
        behind = states[1]
        for stream in range(2):
            turn = stream * TICKS + tick
            partial, scaled, squares = first(me, arrived[stream], norm_gain, weight_in, [behind])
            other = partner(partial, "expert", 0)
            own = second(me, scaled, weight_in)
            hidden = act(me, own, other, squares, model_width)
            hidden_other = partner(hidden, "expert", 0)
            result = third(me, hidden, hidden_other, weight_out)
            behind = result[0]
            arrived[stream] = across(result, ahead)
            ahead = arrived[stream]
        if final:
            for stream in range(2):
                turn = stream * TICKS + tick
                kept, sent = last(me, turn, states[stream], as_columns, arrived[stream], [behind])
                results[stream] = finish(me, kept, partner(sent, "expert", 0))
        else:
            moved[0] = shifted(mix(me, tick, states[0], as_columns, arrived[0], [behind]), "pipe", 1)
            turn_before, state_before = TICKS + tick, states[1]
    return (results[0][None], results[1][None])


def solution(mesh):
    in_specs = (
        P("pipe", "expert", None),
        P("pipe", "expert", None),
        P(None, "expert", None),
        P(None, "expert", None),
        P(None, "pipe", "expert", None),
        P(None, "pipe", "expert", None),
        P(None, "pipe", "expert", None),
        P(None, "pipe", "expert", None),
        P("pipe", None),
        P("pipe", "expert", None, None),
        P("pipe", "expert", None, None),
    )
    out_specs = (P("pipe", "expert", None), P("pipe", "expert", None))
    groups = mesh.shape["expert"] // EXPERTS
    shards = paired_shards if groups == 2 else general_shards
    return jax.shard_map(shards, mesh=mesh, in_specs=in_specs, out_specs=out_specs, check_vma=False)
```

```python
import functools

import jax
import jax.numpy as jnp
from jax import lax
from jax.experimental import pallas as pl
from jax.experimental.pallas import tpu as pltpu
from jax.sharding import PartitionSpec as P

EXPERTS = 4
TICKS = 2
CAP = 18


EPSILON = 1e-06


def partner(shard, axis, apart):
    return lax.ppermute(shard, axis, [(i, i ^ 1 << apart) for i in range(lax.axis_size(axis))])


def shifted(block, axis, distance):
    devices = range(lax.axis_size(axis))
    route = [(i - distance, i) for i in devices if i - distance in devices]
    return lax.ppermute(block, axis, route)


def rms_scaled(joined_rows, gain_row):
    values = joined_rows.astype(jnp.float32)
    scale_row = lax.rsqrt(jnp.mean(values * values, axis=-1, keepdims=True) + EPSILON)
    return (values * scale_row * gain_row[None, :]).astype(jnp.bfloat16)


def slot_tables(joined_routes, joined_shares, batch_count, experts, capacity):
    total_rows = joined_routes.shape[0]
    row_count = total_rows // batch_count
    onehot = (
        joined_routes[:, :, None] == jnp.arange(experts, dtype=jnp.int32)[None, None, :]
    ).astype(jnp.int32)
    per_row = jnp.sum(onehot, axis=1).reshape(batch_count, row_count, experts)
    before = (jnp.cumsum(per_row, axis=1) - per_row).reshape(total_rows, experts)
    slot_of = jnp.sum(onehot * before[:, None, :], axis=2)
    offset = jnp.arange(total_rows, dtype=jnp.int32) // row_count * capacity
    slot_of = slot_of + offset[:, None]
    slot_ids = jnp.arange(batch_count * capacity, dtype=jnp.int32)
    slot_hit = (slot_of[:, :, None] == slot_ids[None, None, :]).astype(jnp.float32)
    onehot_float = onehot.astype(jnp.float32)
    placement = jnp.einsum("rke,rkc->ecr", onehot_float, slot_hit, precision=lax.Precision.HIGHEST)
    weighted = jnp.einsum(
        "rke,rkc->rec",
        onehot_float * joined_shares[:, :, None],
        slot_hit,
        precision=lax.Precision.HIGHEST,
    )
    return (placement, weighted)


def halving_sum(partial_value, groups, halved_bits):
    row_count = partial_value.shape[0]
    slice_width = partial_value.shape[1] // (2 * groups)
    holding = partial_value.reshape(row_count, 2, groups, slice_width)
    member_index = lax.axis_index("expert")
    held_count = groups
    for bit_index in range(halved_bits):
        own_bit = member_index >> bit_index & 1
        reshaped = holding.reshape(row_count, 2, held_count // 2, 2, slice_width)
        kept_half = lax.dynamic_index_in_dim(reshaped, own_bit, 3, keepdims=False)
        sent_half = lax.dynamic_index_in_dim(reshaped, 1 - own_bit, 3, keepdims=False)
        holding = kept_half + partner(sent_half, "expert", bit_index)
        held_count = held_count // 2
    holding = holding + partner(holding, "expert", halved_bits)
    return (holding[:, 0], holding[:, 1])


def doubling_gather(own_piece, gathered_bits):
    row_count, held_count, slice_width = own_piece.shape
    holding = own_piece
    member_index = lax.axis_index("expert")
    for bit_index in reversed(range(gathered_bits)):
        own_bit = member_index >> bit_index & 1
        arrived = partner(holding, "expert", bit_index)
        first_half = jnp.where(own_bit == 0, holding, arrived)
        second_half = jnp.where(own_bit == 0, arrived, holding)
        stacked = jnp.stack([first_half, second_half], axis=2)
        holding = stacked.reshape(row_count, -1, slice_width)
    return holding.reshape(row_count, -1)


def expert_layer(batch_list, route_list, share_list, gain_row, weight_in, weight_out):
    batch_count = len(batch_list)
    row_count = batch_list[0].shape[0]
    model_width = batch_list[0].shape[1]
    groups = lax.axis_size("expert") // EXPERTS
    bit_count = groups.bit_length() - 1
    halved_bits = bit_count - 1
    feat_width = model_width // groups
    joined_rows = batch_list[0]
    joined_routes = route_list[0]
    joined_shares = share_list[0]
    normed = rms_scaled(joined_rows, gain_row)
    placement, weighted = slot_tables(joined_routes, joined_shares, batch_count, EXPERTS, CAP)
    total_rows = batch_count * row_count
    normed_split = normed.reshape(total_rows, groups, feat_width)
    outgoing = jnp.einsum(
        "ecr,rwf->ewcf",
        placement.astype(jnp.bfloat16),
        normed_split,
        preferred_element_type=jnp.float32,
    ).astype(jnp.bfloat16)
    outgoing = outgoing.reshape(EXPERTS * groups, batch_count * CAP, feat_width)
    arrived = lax.all_to_all(outgoing, "expert", split_axis=0, concat_axis=0, tiled=True)
    sources, slot_count, block_width = arrived.shape
    flat_rows = arrived.reshape(sources * slot_count, block_width)
    partial_value = jnp.dot(flat_rows, weight_in, preferred_element_type=jnp.float32)
    gate_part, up_part = halving_sum(partial_value, groups, halved_bits)
    own_piece = (jax.nn.silu(gate_part) * up_part).astype(jnp.bfloat16)
    hidden = doubling_gather(own_piece, halved_bits)
    result = jnp.dot(hidden, weight_out, preferred_element_type=jnp.float32).astype(jnp.bfloat16)
    returned = lax.all_to_all(
        result.reshape(sources, slot_count, block_width),
        "expert",
        split_axis=0,
        concat_axis=0,
        tiled=True,
    )
    returned_split = returned.reshape(EXPERTS, groups, batch_count * CAP, feat_width).astype(
        jnp.float32
    )
    mixed = jnp.einsum(
        "rec,ewcf->rwf", weighted, returned_split, precision=lax.Precision.HIGHEST
    ).reshape(total_rows, model_width)
    output = (joined_rows.astype(jnp.float32) + mixed).astype(jnp.bfloat16)
    return [output]


def general_shards(
    east_batch,
    west_batch,
    east_entering,
    west_entering,
    east_experts,
    west_experts,
    east_gates,
    west_gates,
    norm_gain,
    expert_in,
    expert_down,
):
    section_index = lax.axis_index("pipe")
    section_count = lax.axis_size("pipe")
    gain_row = norm_gain[0]
    weight_in = expert_in[0, 0]
    weight_out = expert_down[0, 0]
    east_now = east_batch[0]
    west_now = west_batch[0]
    for tick_index in range(TICKS):
        east_routes = east_experts[tick_index, 0]
        west_routes = west_experts[tick_index, 0]
        east_shares = east_gates[tick_index, 0]
        west_shares = west_gates[tick_index, 0]
        east_now = expert_layer(
            [east_now], [east_routes], [east_shares], gain_row, weight_in, weight_out
        )[0]
        west_now = expert_layer(
            [west_now], [west_routes], [west_shares], gain_row, weight_in, weight_out
        )[0]
        if tick_index + 1 < TICKS:
            moved_east = shifted(east_now, "pipe", 1)
            east_now = jnp.where(section_index == 0, east_entering[tick_index], moved_east)
            moved_west = shifted(west_now, "pipe", -1)
            west_now = jnp.where(
                section_index == section_count - 1, west_entering[tick_index], moved_west
            )
    return (east_now[None], west_now[None])


PARTS = 4
LIMIT = 16 * 2**20


def whole(count):
    return [pl.BlockSpec(memory_space=pltpu.VMEM)] * count


def without(kernel, place, count, *refs):
    kernel(*refs[:place], *refs[place + count:])


def call(kernel, name, out_shape, me, *arrays, after=(), scratch=(), limit=LIMIT):
    several = isinstance(out_shape, list)
    if after:
        kernel = functools.partial(without, kernel, 1 + len(arrays), len(after))
    unread = [pl.BlockSpec(memory_space=pl.ANY)] * len(after)
    return pl.pallas_call(
        kernel,
        out_shape=out_shape,
        in_specs=[pl.BlockSpec(memory_space=pltpu.SMEM)] + whole(len(arrays)) + unread,
        out_specs=whole(len(out_shape)) if several else whole(1)[0],
        scratch_shapes=list(scratch),
        compiler_params=pltpu.CompilerParams(vmem_limit_bytes=limit),
        cost_estimate=pl.CostEstimate(flops=0, bytes_accessed=0, transcendentals=0),
        name=name,
    )(me, *arrays, *after)


def bf16(*shape):
    return jax.ShapeDtypeStruct(shape, jnp.bfloat16)


def f32(*shape):
    return jax.ShapeDtypeStruct(shape, jnp.float32)


def iota(shape, axis):
    return lax.broadcasted_iota(jnp.int32, shape, axis)


def matmul(a, b):
    return jnp.dot(a, b, preferred_element_type=jnp.float32)


def ones_where(condition):
    return condition.astype(jnp.float32).astype(jnp.bfloat16)


def pieces(values):
    high = values.astype(jnp.bfloat16)
    rest = values - high.astype(jnp.float32)
    middle = rest.astype(jnp.bfloat16)
    return high, middle, (rest - middle.astype(jnp.float32)).astype(jnp.bfloat16)


def cut_kernel(me, batch, sent):
    half = sent.shape[1]
    sent[...] = batch[:, pl.ds(pl.multiple_of((1 - me[1]) * half, half), half)]


def cut(me, batch):
    rows, model_width = batch.shape
    return call(cut_kernel, "cut", bf16(rows, model_width // 2), me, batch)


def tables_kernel(me, own, other, as_rows, as_columns):
    rows = own.shape[1]
    total = as_rows.shape[1]
    row_sum = jnp.zeros(as_rows.shape, jnp.float32)
    column_sum = jnp.zeros(as_columns.shape, jnp.float32)
    for source, x in ((own, me[1]), (other, 1 - me[1])):
        token, column = iota((rows, total), 0), iota((rows, total), 1)
        spread = ones_where((column % rows == token) & (column // rows % 2 == x))
        line, lane = iota((total, rows), 0), iota((total, rows), 1)
        gather = ones_where((line % rows == lane) & (line // rows % 2 == x))
        high, middle, low = pieces(source[...])
        row_sum = row_sum + ((matmul(low, spread) + matmul(middle, spread)) + matmul(high, spread))
        turned = [
            lax.dot_general(gather, piece, (((1,), (1,)), ((), ())), preferred_element_type=jnp.float32)
            for piece in (low, middle, high)
        ]
        column_sum = column_sum + ((turned[0] + turned[1]) + turned[2])
    as_rows[...] = row_sum
    as_columns[...] = column_sum


def tables(me, own, other):
    kinds, rows = own.shape
    total = 2 * PARTS * rows
    return call(tables_kernel, "tables", [f32(kinds, total), f32(total, kinds)], me, own, other)


def joined(me, batch, other, state):
    rows, half = other.shape
    kept = batch[:, pl.ds(pl.multiple_of(me[1] * half, half), half)]
    state[pl.ds(pl.multiple_of(me[1] * rows, rows), rows), :] = kept
    state[pl.ds(pl.multiple_of((1 - me[1]) * rows, rows), rows), :] = other[...]


def packed(me, state, table, turn, outs, stacked):
    tokens, half = state.shape
    rows = tokens // 2
    width = half // PARTS
    total = PARTS * tokens
    slots = 2 * CAP
    for part in range(PARTS):
        stacked[part * tokens:(part + 1) * tokens, :] = state[:, part * width:(part + 1) * width]
    expert = me[0] ^ iota((8, total), 0)
    chosen = table[4 * turn:4 * turn + 2, :].astype(jnp.int32)
    named = (chosen[0:1, :] == expert) | (chosen[1:2, :] == expert)
    earlier = (iota((total, total), 0) // rows == iota((total, total), 1) // rows) & (
        iota((total, total), 0) < iota((total, total), 1)
    )
    before = matmul(ones_where(named), ones_where(earlier))
    column = iota((8, total), 1)
    start = column // tokens * slots + column // rows % 2 * CAP
    place = jnp.where(named, start + before.astype(jnp.int32), -1)
    for apart in range(EXPERTS):
        hit = iota((PARTS * slots, total), 0) == place[apart:apart + 1, :]
        outs[apart][...] = matmul(ones_where(hit), stacked[...]).astype(jnp.bfloat16)


def enter_kernel(turn, me, batch, other, table, o0, o1, o2, o3, state, stacked):
    joined(me, batch, other, state)
    packed(me, state, table, turn, (o0, o1, o2, o3), stacked)


def relay_kernel(turn, edge, me, moved, moved_rest, batch, other, table, o0, o1, o2, o3, state, stacked):
    state[:moved.shape[0], :] = moved[...]
    state[moved.shape[0]:, :] = moved_rest[...]

    @pl.when(me[2 + edge] == 1)
    def _():
        joined(me, batch, other, state)

    packed(me, state, table, turn, (o0, o1, o2, o3), stacked)


def pack_shapes(rows, half):
    width = half // PARTS
    outs = [bf16(PARTS * 2 * CAP, width)] * EXPERTS + [bf16(2 * rows, half)]
    return outs, [pltpu.VMEM((PARTS * 2 * rows, width), jnp.bfloat16)]


def enter(me, turn, batch, other, table, after):
    outs, scratch = pack_shapes(*other.shape)
    made = call(functools.partial(enter_kernel, turn), "enter", outs, me, batch, other, table, after=after, scratch=scratch)
    return made[:EXPERTS], made[EXPERTS]


def relay(me, turn, edge, moved, batch, other, table):
    outs, scratch = pack_shapes(*other.shape)
    kernel = functools.partial(relay_kernel, turn, edge)
    made = call(kernel, "relay", outs, me, *moved, batch, other, table, scratch=scratch)
    return made[:EXPERTS], made[EXPERTS]


def load_kernel(me, source, other_source, out, other_out, done):
    copies = [
        pltpu.make_async_copy(source, out, done.at[0]),
        pltpu.make_async_copy(other_source, other_out, done.at[1]),
    ]
    for copy in copies:
        copy.start()
    for copy in copies:
        copy.wait()


def load(me, weight, other_weight, after):
    arrays = [weight, other_weight]
    kernel = functools.partial(without, load_kernel, 3, len(after))
    return pl.pallas_call(
        kernel,
        out_shape=[bf16(*array.shape) for array in arrays],
        in_specs=[pl.BlockSpec(memory_space=pltpu.SMEM)] + [pl.BlockSpec(memory_space=pltpu.HBM)] * 2
        + [pl.BlockSpec(memory_space=pl.ANY)] * len(after),
        out_specs=whole(2),
        scratch_shapes=[pltpu.SemaphoreType.DMA((2,))],
        compiler_params=pltpu.CompilerParams(vmem_limit_bytes=LIMIT),
        cost_estimate=pl.CostEstimate(flops=0, bytes_accessed=0, transcendentals=0),
        name="load",
    )(me, *arrays, *after)


def first_kernel(me, r0, r1, r2, r3, gain, weight, message, rows_out, squares, stacked):
    slots = 2 * CAP
    block = PARTS * slots
    width = r0.shape[1]
    for apart, ref in enumerate((r0, r1, r2, r3)):
        stacked[apart * block:(apart + 1) * block, :] = ref[...]
    row = iota((block, EXPERTS * block), 0)
    column = iota((block, EXPERTS * block), 1)
    total = jnp.zeros((block, 1), jnp.float32)
    for part in range(PARTS):
        source = row // slots * block + part * slots + row % slots
        values = matmul(ones_where(column == source), stacked[...])
        total = total + jnp.sum(values * values, axis=1, keepdims=True)
        start = pl.multiple_of(me[1] * PARTS * width + part * width, width)
        scaled = values * gain[:, pl.ds(start, width)]
        rows_out[:, part * width:(part + 1) * width] = scaled.astype(jnp.bfloat16)
    squares[...] = jnp.broadcast_to(total, squares.shape)
    units = weight.shape[1] // 4
    lane = iota(squares.shape, 1)
    high, middle, low = [piece.astype(jnp.float32) for piece in pieces(total)]
    sent = jnp.where(lane == 0, high, jnp.where(lane == 1, middle, jnp.where(lane == 2, low, 0.0)))
    turned = lax.dot_general(
        sent.astype(jnp.bfloat16),
        ones_where(iota((block, block), 0) == iota((block, block), 1)),
        (((0,), (0,)), ((), ())),
        preferred_element_type=jnp.float32,
    )
    message[block:, :] = jnp.zeros((message.shape[0] - block, units), jnp.bfloat16)
    message[block:, :block] = turned[:message.shape[0] - block, :].astype(jnp.bfloat16)
    start = pl.multiple_of(units * (1 - me[1]), units)
    message[:block, :] = matmul(rows_out[...], weight[:, pl.ds(start, units)]).astype(jnp.bfloat16)


def first(me, received, gain, weight, after):
    block, width = received[0].shape
    half, both = weight.shape
    outs = [bf16(block + 16, both // 4), bf16(block, half), f32(block, 128)]
    scratch = [pltpu.VMEM((EXPERTS * block, width), jnp.bfloat16)]
    return call(first_kernel, "first", outs, me, *received, gain, weight, after=after, scratch=scratch)


def second_kernel(me, rows_in, weight, message):
    units = weight.shape[1] // 4
    start = pl.multiple_of(units * (3 - me[1]), units)
    message[...] = matmul(rows_in[...], weight[:, pl.ds(start, units)]).astype(jnp.bfloat16)


def second(me, rows_in, weight):
    return call(second_kernel, "second", bf16(rows_in.shape[0], weight.shape[1] // 4), me, rows_in, weight)


def own_kernel(me, rows_in, weight, own):
    units = weight.shape[1] // 4
    for kind in range(2):
        start = pl.multiple_of(units * (2 * kind + me[1]), units)
        own[:, kind * units:(kind + 1) * units] = matmul(rows_in[...], weight[:, pl.ds(start, units)])


def own_half(me, rows_in, weight):
    return call(own_kernel, "own", f32(rows_in.shape[0], weight.shape[1] // 2), me, rows_in, weight)


def act_kernel(model_width, me, own, gates, ups, squares, h0, h1):
    block, both = own.shape
    units = both // 2
    pair = lax.dot_general(
        ones_where(iota((block, block), 0) == iota((block, block), 1)),
        gates[block:, :block],
        (((1,), (1,)), ((), ())),
        preferred_element_type=jnp.float32,
    )
    mean = (squares[:, 0:1] + ((pair[:, 2:3] + pair[:, 1:2]) + pair[:, 0:1])) / model_width
    scale = lax.rsqrt(mean + EPSILON)
    gate = (own[:, :units] + gates[:block, :].astype(jnp.float32)) * scale
    up = (own[:, units:] + ups[...].astype(jnp.float32)) * scale
    hidden = (gate / (1.0 + jnp.exp(-gate)) * up).astype(jnp.bfloat16)
    h0[...] = hidden[:, :units // 2]
    h1[...] = hidden[:, units // 2:]


def act(me, own, gates, ups, squares, model_width):
    block, both = own.shape
    outs = [bf16(block, both // 4)] * 2
    return call(functools.partial(act_kernel, model_width), "act", outs, me, own, gates, ups, squares)


def third_kernel(me, h0, h1, t0, t1, weight, *refs):
    o0, o1, o2, o3, hidden, stacked = refs
    slots = 2 * CAP
    block, units = hidden.shape
    size = units // 4
    width = o0.shape[1]
    for index, refs in enumerate(((h0, h1), (t0, t1))):
        for place, ref in enumerate(refs):
            start = ((me[1] ^ index) * 2 + place) * size
            hidden[:, pl.ds(pl.multiple_of(start, size), size)] = ref[...]
    for part in range(PARTS):
        result = matmul(hidden[...], weight[:, part * width:(part + 1) * width])
        stacked[part * block:(part + 1) * block, :] = result.astype(jnp.bfloat16)
    row = iota((block, PARTS * block), 0)
    column = iota((block, PARTS * block), 1)
    for apart, out in enumerate((o0, o1, o2, o3)):
        source = row // slots * block + apart * slots + row % slots
        out[...] = matmul(ones_where(column == source), stacked[...]).astype(jnp.bfloat16)


def third(me, hidden, hidden_other, weight):
    block = hidden[0].shape[0]
    units, half = weight.shape
    width = half // PARTS
    outs = [bf16(block, width)] * EXPERTS
    scratch = [pltpu.VMEM((block, units), jnp.bfloat16), pltpu.VMEM((PARTS * block, width), jnp.bfloat16)]
    return call(third_kernel, "third", outs, me, *hidden, *hidden_other, weight, scratch=scratch)


def mixed_parts(me, table, turn, received, tokens):
    rows = tokens // 2
    width = received[0].shape[1]
    total = PARTS * tokens
    slots = 2 * CAP
    expert = me[0] ^ iota((total, 128), 1)
    chosen = table[:, 4 * turn:4 * turn + 2].astype(jnp.int32)
    share = table[:, 4 * turn + 2:4 * turn + 4]
    hits = [chosen[:, k:k + 1] == expert for k in range(2)]
    weight = jnp.where(hits[0], share[:, 0:1], 0.0) + jnp.where(hits[1], share[:, 1:2], 0.0)
    named = hits[0] | hits[1]
    earlier = (iota((total, total), 0) // rows == iota((total, total), 1) // rows) & (
        iota((total, total), 0) > iota((total, total), 1)
    )
    before = matmul(ones_where(earlier), ones_where(named))
    line = iota((total, 128), 0)
    start = line // tokens * slots + line // rows % 2 * CAP
    place = jnp.where(named, start + before.astype(jnp.int32), -1)
    mixed = jnp.zeros((total, width), jnp.float32)
    for apart, ref in enumerate(received):
        hit = iota((total, PARTS * slots), 1) == place[:, apart:apart + 1]
        spread = jnp.where(hit, weight[:, apart:apart + 1], 0.0)
        high = spread.astype(jnp.bfloat16)
        low = (spread - high.astype(jnp.float32)).astype(jnp.bfloat16)
        mixed = mixed + matmul(high, ref[...]) + matmul(low, ref[...])
    return mixed


def mix_kernel(turn, me, state, table, r0, r1, r2, r3, out):
    tokens = state.shape[0]
    width = r0.shape[1]
    mixed = mixed_parts(me, table, turn, (r0, r1, r2, r3), tokens)
    for part in range(PARTS):
        span = slice(part * width, (part + 1) * width)
        summed = state[:, span].astype(jnp.float32) + mixed[part * tokens:(part + 1) * tokens, :]
        out[:, span] = summed.astype(jnp.bfloat16)


def halves_kernel(turn, me, state, table, *refs):
    *received, upper, lower, result = refs
    mix_kernel(turn, me, state, table, *received, result)
    upper[...] = result[:upper.shape[0], :]
    lower[...] = result[upper.shape[0]:, :]


def mix(me, turn, state, table, received, after):
    kernel = functools.partial(halves_kernel, turn)
    tokens, half = state.shape
    outs = [bf16(tokens // 2, half)] * 2
    scratch = [pltpu.VMEM(state.shape, jnp.bfloat16)]
    return call(kernel, "mix", outs, me, state, table, *received, after=after, scratch=scratch)


def last_kernel(turn, me, state, table, r0, r1, r2, r3, kept, sent, result):
    rows = kept.shape[0]
    mix_kernel(turn, me, state, table, r0, r1, r2, r3, result)
    kept[...] = result[pl.ds(pl.multiple_of(me[1] * rows, rows), rows), :]
    sent[...] = result[pl.ds(pl.multiple_of((1 - me[1]) * rows, rows), rows), :]


def last(me, turn, state, table, received, after):
    tokens, half = state.shape
    outs = [bf16(tokens // 2, half)] * 2
    scratch = [pltpu.VMEM(state.shape, jnp.bfloat16)]
    return call(functools.partial(last_kernel, turn), "last", outs, me, state, table, *received, after=after, scratch=scratch)


def finish_kernel(me, kept, other, out):
    half = kept.shape[1]
    out[:, pl.ds(pl.multiple_of(me[1] * half, half), half)] = kept[...]
    out[:, pl.ds(pl.multiple_of((1 - me[1]) * half, half), half)] = other[...]


def finish(me, kept, other):
    return call(finish_kernel, "finish", bf16(kept.shape[0], 2 * kept.shape[1]), me, kept, other)


def along(block, apart):
    return lax.ppermute(block, "expert", [(i, i ^ 2 * apart) for i in range(lax.axis_size("expert"))])


def across(blocks, behind=None):
    own, near, two, three = blocks
    if behind is not None:
        near, two, three, *behind[2:] = lax.optimization_barrier((near, two, three, *behind[2:]))
    two, three = along(two, 2), along(three, 3)
    return [own, along(near, 1), two, three]


def paired_shards(
    east_batch,
    west_batch,
    east_entering,
    west_entering,
    east_experts,
    west_experts,
    east_gates,
    west_gates,
    norm_gain,
    expert_in,
    expert_down,
):
    section_index = lax.axis_index("pipe")
    section_count = lax.axis_size("pipe")
    member = lax.axis_index("expert")
    edges = [section_index == 0, section_index == section_count - 1]
    me = jnp.stack([member // 2, member % 2, *edges]).astype(jnp.int32)
    rows, model_width = east_batch.shape[1:]
    kinds = [
        jnp.swapaxes(array[tick, 0], 0, 1).astype(jnp.float32)
        for experts, gates in ((east_experts, east_gates), (west_experts, west_gates))
        for tick in range(TICKS)
        for array in (experts, gates)
    ]
    lists = jnp.concatenate(kinds, axis=0)

    batches = [east_batch[0], west_batch[0]]
    entering = [east_entering[0], west_entering[0]]
    batches_other = [partner(cut(me, batch), "expert", 0) for batch in batches]
    as_rows, as_columns = tables(me, lists, partner(lists, "expert", 0))
    entering_other = [partner(cut(me, batch), "expert", 0) for batch in entering]
    moved = [None, None]
    results = [None, None]
    states = [None, None]
    ahead = None
    for tick in range(TICKS):
        final = tick + 1 == TICKS
        arrived = [None, None]
        for stream in range(2):
            turn = stream * TICKS + tick
            if tick == 0:
                after = []
                if stream == 1:
                    weight_in, weight_out = load(me, expert_in[0, 0], expert_down[0, 0], [states[0]])
                    after = [weight_in, *entering_other]
                sent, states[stream] = enter(me, turn, batches[stream], batches_other[stream], as_rows, after)
            else:
                sent, states[stream] = relay(
                    me, turn, stream, moved[stream], entering[stream], entering_other[stream], as_rows
                )
                if stream == 0:
                    pieces_now = mix(me, turn_before, state_before, as_columns, ahead, [sent[0]])
                    moved[1] = [shifted(piece, "pipe", -1) for piece in pieces_now]
            arrived[stream] = across(sent, ahead)
            ahead = arrived[stream]
        behind = states[1]
        for stream in range(2):
            turn = stream * TICKS + tick
            message, scaled, squares = first(me, arrived[stream], norm_gain, weight_in, [behind])
            gates = partner(message, "expert", 0)
            ups = partner(second(me, scaled, weight_in), "expert", 0)
            own = own_half(me, scaled, weight_in)
            hidden = act(me, own, gates, ups, squares, model_width)
            hidden_other = [partner(half, "expert", 0) for half in hidden]
            result = third(me, hidden, hidden_other, weight_out)
            behind = result[0]
            arrived[stream] = across(result, ahead)
            ahead = arrived[stream]
        if final:
            for stream in range(2):
                turn = stream * TICKS + tick
                kept, sent = last(me, turn, states[stream], as_columns, arrived[stream], [behind])
                results[stream] = finish(me, kept, partner(sent, "expert", 0))
        else:
            pieces_now = mix(me, tick, states[0], as_columns, arrived[0], [behind])
            moved[0] = [shifted(piece, "pipe", 1) for piece in pieces_now]
            turn_before, state_before = TICKS + tick, states[1]
    return (results[0][None], results[1][None])


def solution(mesh):
    in_specs = (
        P("pipe", "expert", None),
        P("pipe", "expert", None),
        P(None, "expert", None),
        P(None, "expert", None),
        P(None, "pipe", "expert", None),
        P(None, "pipe", "expert", None),
        P(None, "pipe", "expert", None),
        P(None, "pipe", "expert", None),
        P("pipe", None),
        P("pipe", "expert", None, None),
        P("pipe", "expert", None, None),
    )
    out_specs = (P("pipe", "expert", None), P("pipe", "expert", None))
    groups = mesh.shape["expert"] // EXPERTS
    shards = paired_shards if groups == 2 else general_shards
    return jax.shard_map(shards, mesh=mesh, in_specs=in_specs, out_specs=out_specs, check_vma=False)
```

```python
import functools

import jax
import jax.numpy as jnp
from jax import lax
from jax.experimental import pallas as pl
from jax.experimental.pallas import tpu as pltpu
from jax.sharding import PartitionSpec as P

EXPERTS = 4
TICKS = 2
CAP = 18


EPSILON = 1e-06


def partner(shard, axis, apart):
    return lax.ppermute(shard, axis, [(i, i ^ 1 << apart) for i in range(lax.axis_size(axis))])


def shifted(block, axis, distance):
    devices = range(lax.axis_size(axis))
    route = [(i - distance, i) for i in devices if i - distance in devices]
    return lax.ppermute(block, axis, route)


def rms_scaled(joined_rows, gain_row):
    values = joined_rows.astype(jnp.float32)
    scale_row = lax.rsqrt(jnp.mean(values * values, axis=-1, keepdims=True) + EPSILON)
    return (values * scale_row * gain_row[None, :]).astype(jnp.bfloat16)


def slot_tables(joined_routes, joined_shares, batch_count, experts, capacity):
    total_rows = joined_routes.shape[0]
    row_count = total_rows // batch_count
    onehot = (
        joined_routes[:, :, None] == jnp.arange(experts, dtype=jnp.int32)[None, None, :]
    ).astype(jnp.int32)
    per_row = jnp.sum(onehot, axis=1).reshape(batch_count, row_count, experts)
    before = (jnp.cumsum(per_row, axis=1) - per_row).reshape(total_rows, experts)
    slot_of = jnp.sum(onehot * before[:, None, :], axis=2)
    offset = jnp.arange(total_rows, dtype=jnp.int32) // row_count * capacity
    slot_of = slot_of + offset[:, None]
    slot_ids = jnp.arange(batch_count * capacity, dtype=jnp.int32)
    slot_hit = (slot_of[:, :, None] == slot_ids[None, None, :]).astype(jnp.float32)
    onehot_float = onehot.astype(jnp.float32)
    placement = jnp.einsum("rke,rkc->ecr", onehot_float, slot_hit, precision=lax.Precision.HIGHEST)
    weighted = jnp.einsum(
        "rke,rkc->rec",
        onehot_float * joined_shares[:, :, None],
        slot_hit,
        precision=lax.Precision.HIGHEST,
    )
    return (placement, weighted)


def halving_sum(partial_value, groups, halved_bits):
    row_count = partial_value.shape[0]
    slice_width = partial_value.shape[1] // (2 * groups)
    holding = partial_value.reshape(row_count, 2, groups, slice_width)
    member_index = lax.axis_index("expert")
    held_count = groups
    for bit_index in range(halved_bits):
        own_bit = member_index >> bit_index & 1
        reshaped = holding.reshape(row_count, 2, held_count // 2, 2, slice_width)
        kept_half = lax.dynamic_index_in_dim(reshaped, own_bit, 3, keepdims=False)
        sent_half = lax.dynamic_index_in_dim(reshaped, 1 - own_bit, 3, keepdims=False)
        holding = kept_half + partner(sent_half, "expert", bit_index)
        held_count = held_count // 2
    holding = holding + partner(holding, "expert", halved_bits)
    return (holding[:, 0], holding[:, 1])


def doubling_gather(own_piece, gathered_bits):
    row_count, held_count, slice_width = own_piece.shape
    holding = own_piece
    member_index = lax.axis_index("expert")
    for bit_index in reversed(range(gathered_bits)):
        own_bit = member_index >> bit_index & 1
        arrived = partner(holding, "expert", bit_index)
        first_half = jnp.where(own_bit == 0, holding, arrived)
        second_half = jnp.where(own_bit == 0, arrived, holding)
        stacked = jnp.stack([first_half, second_half], axis=2)
        holding = stacked.reshape(row_count, -1, slice_width)
    return holding.reshape(row_count, -1)


def expert_layer(batch_list, route_list, share_list, gain_row, weight_in, weight_out):
    batch_count = len(batch_list)
    row_count = batch_list[0].shape[0]
    model_width = batch_list[0].shape[1]
    groups = lax.axis_size("expert") // EXPERTS
    bit_count = groups.bit_length() - 1
    halved_bits = bit_count - 1
    feat_width = model_width // groups
    joined_rows = batch_list[0]
    joined_routes = route_list[0]
    joined_shares = share_list[0]
    normed = rms_scaled(joined_rows, gain_row)
    placement, weighted = slot_tables(joined_routes, joined_shares, batch_count, EXPERTS, CAP)
    total_rows = batch_count * row_count
    normed_split = normed.reshape(total_rows, groups, feat_width)
    outgoing = jnp.einsum(
        "ecr,rwf->ewcf",
        placement.astype(jnp.bfloat16),
        normed_split,
        preferred_element_type=jnp.float32,
    ).astype(jnp.bfloat16)
    outgoing = outgoing.reshape(EXPERTS * groups, batch_count * CAP, feat_width)
    arrived = lax.all_to_all(outgoing, "expert", split_axis=0, concat_axis=0, tiled=True)
    sources, slot_count, block_width = arrived.shape
    flat_rows = arrived.reshape(sources * slot_count, block_width)
    partial_value = jnp.dot(flat_rows, weight_in, preferred_element_type=jnp.float32)
    gate_part, up_part = halving_sum(partial_value, groups, halved_bits)
    own_piece = (jax.nn.silu(gate_part) * up_part).astype(jnp.bfloat16)
    hidden = doubling_gather(own_piece, halved_bits)
    result = jnp.dot(hidden, weight_out, preferred_element_type=jnp.float32).astype(jnp.bfloat16)
    returned = lax.all_to_all(
        result.reshape(sources, slot_count, block_width),
        "expert",
        split_axis=0,
        concat_axis=0,
        tiled=True,
    )
    returned_split = returned.reshape(EXPERTS, groups, batch_count * CAP, feat_width).astype(
        jnp.float32
    )
    mixed = jnp.einsum(
        "rec,ewcf->rwf", weighted, returned_split, precision=lax.Precision.HIGHEST
    ).reshape(total_rows, model_width)
    output = (joined_rows.astype(jnp.float32) + mixed).astype(jnp.bfloat16)
    return [output]


def general_shards(
    east_batch,
    west_batch,
    east_entering,
    west_entering,
    east_experts,
    west_experts,
    east_gates,
    west_gates,
    norm_gain,
    expert_in,
    expert_down,
):
    section_index = lax.axis_index("pipe")
    section_count = lax.axis_size("pipe")
    gain_row = norm_gain[0]
    weight_in = expert_in[0, 0]
    weight_out = expert_down[0, 0]
    east_now = east_batch[0]
    west_now = west_batch[0]
    for tick_index in range(TICKS):
        east_routes = east_experts[tick_index, 0]
        west_routes = west_experts[tick_index, 0]
        east_shares = east_gates[tick_index, 0]
        west_shares = west_gates[tick_index, 0]
        east_now = expert_layer(
            [east_now], [east_routes], [east_shares], gain_row, weight_in, weight_out
        )[0]
        west_now = expert_layer(
            [west_now], [west_routes], [west_shares], gain_row, weight_in, weight_out
        )[0]
        if tick_index + 1 < TICKS:
            moved_east = shifted(east_now, "pipe", 1)
            east_now = jnp.where(section_index == 0, east_entering[tick_index], moved_east)
            moved_west = shifted(west_now, "pipe", -1)
            west_now = jnp.where(
                section_index == section_count - 1, west_entering[tick_index], moved_west
            )
    return (east_now[None], west_now[None])


PARTS = 4
LIMIT = 16 * 2**20


def whole(count):
    return [pl.BlockSpec(memory_space=pltpu.VMEM)] * count


def without(kernel, place, count, *refs):
    kernel(*refs[:place], *refs[place + count:])


def call(kernel, name, out_shape, me, *arrays, after=(), scratch=(), limit=LIMIT):
    several = isinstance(out_shape, list)
    if after:
        kernel = functools.partial(without, kernel, 1 + len(arrays), len(after))
    unread = [pl.BlockSpec(memory_space=pl.ANY)] * len(after)
    return pl.pallas_call(
        kernel,
        out_shape=out_shape,
        in_specs=[pl.BlockSpec(memory_space=pltpu.SMEM)] + whole(len(arrays)) + unread,
        out_specs=whole(len(out_shape)) if several else whole(1)[0],
        scratch_shapes=list(scratch),
        compiler_params=pltpu.CompilerParams(vmem_limit_bytes=limit),
        cost_estimate=pl.CostEstimate(flops=0, bytes_accessed=0, transcendentals=0),
        name=name,
    )(me, *arrays, *after)


def bf16(*shape):
    return jax.ShapeDtypeStruct(shape, jnp.bfloat16)


def f32(*shape):
    return jax.ShapeDtypeStruct(shape, jnp.float32)


def iota(shape, axis):
    return lax.broadcasted_iota(jnp.int32, shape, axis)


def matmul(a, b):
    return jnp.dot(a, b, preferred_element_type=jnp.float32)


def ones_where(condition):
    return condition.astype(jnp.float32).astype(jnp.bfloat16)


def pieces(values):
    high = values.astype(jnp.bfloat16)
    rest = values - high.astype(jnp.float32)
    middle = rest.astype(jnp.bfloat16)
    return high, middle, (rest - middle.astype(jnp.float32)).astype(jnp.bfloat16)


def cut_kernel(me, batch, sent):
    half = sent.shape[1]
    sent[...] = batch[:, pl.ds(pl.multiple_of((1 - me[1]) * half, half), half)]


def cut(me, batch):
    rows, model_width = batch.shape
    return call(cut_kernel, "cut", bf16(rows, model_width // 2), me, batch)


def tables_kernel(me, own, other, as_rows, as_columns):
    rows = own.shape[1]
    total = as_rows.shape[1]
    row_sum = jnp.zeros(as_rows.shape, jnp.float32)
    column_sum = jnp.zeros(as_columns.shape, jnp.float32)
    for source, x in ((own, me[1]), (other, 1 - me[1])):
        token, column = iota((rows, total), 0), iota((rows, total), 1)
        spread = ones_where((column % rows == token) & (column // rows % 2 == x))
        line, lane = iota((total, rows), 0), iota((total, rows), 1)
        gather = ones_where((line % rows == lane) & (line // rows % 2 == x))
        high, middle, low = pieces(source[...])
        row_sum = row_sum + ((matmul(low, spread) + matmul(middle, spread)) + matmul(high, spread))
        turned = [
            lax.dot_general(gather, piece, (((1,), (1,)), ((), ())), preferred_element_type=jnp.float32)
            for piece in (low, middle, high)
        ]
        column_sum = column_sum + ((turned[0] + turned[1]) + turned[2])
    as_rows[...] = row_sum
    as_columns[...] = column_sum


def tables(me, own, other):
    kinds, rows = own.shape
    total = 2 * PARTS * rows
    return call(tables_kernel, "tables", [f32(kinds, total), f32(total, kinds)], me, own, other)


def joined(me, batch, other, state):
    rows, half = other.shape
    kept = batch[:, pl.ds(pl.multiple_of(me[1] * half, half), half)]
    state[pl.ds(pl.multiple_of(me[1] * rows, rows), rows), :] = kept
    state[pl.ds(pl.multiple_of((1 - me[1]) * rows, rows), rows), :] = other[...]


def packed(me, state, table, turn, outs, stacked):
    tokens, half = state.shape
    rows = tokens // 2
    width = half // PARTS
    total = PARTS * tokens
    slots = 2 * CAP
    for part in range(PARTS):
        stacked[part * tokens:(part + 1) * tokens, :] = state[:, part * width:(part + 1) * width]
    expert = me[0] ^ iota((8, total), 0)
    chosen = table[4 * turn:4 * turn + 2, :].astype(jnp.int32)
    named = (chosen[0:1, :] == expert) | (chosen[1:2, :] == expert)
    earlier = (iota((total, total), 0) // rows == iota((total, total), 1) // rows) & (
        iota((total, total), 0) < iota((total, total), 1)
    )
    before = matmul(ones_where(named), ones_where(earlier))
    column = iota((8, total), 1)
    start = column // tokens * slots + column // rows % 2 * CAP
    place = jnp.where(named, start + before.astype(jnp.int32), -1)
    for apart in range(EXPERTS):
        hit = iota((PARTS * slots, total), 0) == place[apart:apart + 1, :]
        outs[apart][...] = matmul(ones_where(hit), stacked[...]).astype(jnp.bfloat16)


def enter_kernel(turn, me, batch, other, table, o0, o1, o2, o3, state, stacked):
    joined(me, batch, other, state)
    packed(me, state, table, turn, (o0, o1, o2, o3), stacked)


def relay_kernel(turn, edge, me, moved, moved_rest, batch, other, table, o0, o1, o2, o3, state, stacked):
    state[:moved.shape[0], :] = moved[...]
    state[moved.shape[0]:, :] = moved_rest[...]

    @pl.when(me[2 + edge] == 1)
    def _():
        joined(me, batch, other, state)

    packed(me, state, table, turn, (o0, o1, o2, o3), stacked)


def pack_shapes(rows, half):
    width = half // PARTS
    outs = [bf16(PARTS * 2 * CAP, width)] * EXPERTS + [bf16(2 * rows, half)]
    return outs, [pltpu.VMEM((PARTS * 2 * rows, width), jnp.bfloat16)]


def enter(me, turn, batch, other, table, after):
    outs, scratch = pack_shapes(*other.shape)
    made = call(functools.partial(enter_kernel, turn), "enter", outs, me, batch, other, table, after=after, scratch=scratch)
    return made[:EXPERTS], made[EXPERTS]


def relay(me, turn, edge, moved, batch, other, table):
    outs, scratch = pack_shapes(*other.shape)
    kernel = functools.partial(relay_kernel, turn, edge)
    made = call(kernel, "relay", outs, me, *moved, batch, other, table, scratch=scratch)
    return made[:EXPERTS], made[EXPERTS]


def load_kernel(me, source, other_source, out, other_out, done):
    copies = [
        pltpu.make_async_copy(source, out, done.at[0]),
        pltpu.make_async_copy(other_source, other_out, done.at[1]),
    ]
    for copy in copies:
        copy.start()
    for copy in copies:
        copy.wait()


def load(me, weight, other_weight, after):
    arrays = [weight, other_weight]
    kernel = functools.partial(without, load_kernel, 3, len(after))
    return pl.pallas_call(
        kernel,
        out_shape=[bf16(*array.shape) for array in arrays],
        in_specs=[pl.BlockSpec(memory_space=pltpu.SMEM)] + [pl.BlockSpec(memory_space=pltpu.HBM)] * 2
        + [pl.BlockSpec(memory_space=pl.ANY)] * len(after),
        out_specs=whole(2),
        scratch_shapes=[pltpu.SemaphoreType.DMA((2,))],
        compiler_params=pltpu.CompilerParams(vmem_limit_bytes=LIMIT),
        cost_estimate=pl.CostEstimate(flops=0, bytes_accessed=0, transcendentals=0),
        name="load",
    )(me, *arrays, *after)


def first_kernel(me, r0, r1, r2, r3, gain, weight, gates, ups, rows_out, squares):
    slots = 2 * CAP
    block, width = r0.shape
    units = weight.shape[1] // 4
    held = [ref[...].astype(jnp.float32) for ref in (r0, r1, r2, r3)]
    total = jnp.zeros((block, 1), jnp.float32)
    for part in range(PARTS):
        values = jnp.concatenate([rows[part * slots:(part + 1) * slots, :] for rows in held], axis=0)
        total = total + jnp.sum(values * values, axis=1, keepdims=True)
        start = pl.multiple_of(me[1] * PARTS * width + part * width, width)
        scaled = values * gain[:, pl.ds(start, width)]
        rows_out[:, part * width:(part + 1) * width] = scaled.astype(jnp.bfloat16)
    squares[...] = jnp.broadcast_to(total, squares.shape)
    lane = iota(squares.shape, 1)
    high, middle, low = [piece.astype(jnp.float32) for piece in pieces(total)]
    sent = jnp.where(lane == 0, high, jnp.where(lane == 1, middle, jnp.where(lane == 2, low, 0.0)))
    turned = lax.dot_general(
        sent.astype(jnp.bfloat16),
        ones_where(iota((block, block), 0) == iota((block, block), 1)),
        (((0,), (0,)), ((), ())),
        preferred_element_type=jnp.float32,
    )
    extra = gates.shape[0] - block
    gates[block:, :] = jnp.zeros((extra, units), jnp.bfloat16)
    gates[block:, :block] = turned[:extra, :].astype(jnp.bfloat16)
    for kind in range(2):
        start = pl.multiple_of(units * (2 * kind + 1 - me[1]), units)
        columns = matmul(rows_out[...], weight[:, pl.ds(start, units)]).astype(jnp.bfloat16)
        (gates, ups)[kind][:block, :] = columns


def first(me, received, gain, weight, after):
    block, width = received[0].shape
    half, both = weight.shape
    outs = [bf16(block + 16, both // 4), bf16(block, both // 4), bf16(block, half), f32(block, 128)]
    return call(first_kernel, "first", outs, me, *received, gain, weight, after=after)


def own_kernel(me, rows_in, weight, own):
    units = weight.shape[1] // 4
    for kind in range(2):
        start = pl.multiple_of(units * (2 * kind + me[1]), units)
        own[:, kind * units:(kind + 1) * units] = matmul(rows_in[...], weight[:, pl.ds(start, units)])


def own_half(me, rows_in, weight):
    return call(own_kernel, "own", f32(rows_in.shape[0], weight.shape[1] // 2), me, rows_in, weight)


def act_kernel(model_width, me, own, gates, ups, squares, h0, h1):
    block, both = own.shape
    units = both // 2
    pair = lax.dot_general(
        ones_where(iota((block, block), 0) == iota((block, block), 1)),
        gates[block:, :block],
        (((1,), (1,)), ((), ())),
        preferred_element_type=jnp.float32,
    )
    mean = (squares[:, 0:1] + ((pair[:, 2:3] + pair[:, 1:2]) + pair[:, 0:1])) / model_width
    scale = lax.rsqrt(mean + EPSILON)
    gate = (own[:, :units] + gates[:block, :].astype(jnp.float32)) * scale
    up = (own[:, units:] + ups[...].astype(jnp.float32)) * scale
    hidden = (gate / (1.0 + jnp.exp(-gate)) * up).astype(jnp.bfloat16)
    h0[...] = hidden[:, :units // 2]
    h1[...] = hidden[:, units // 2:]


def act(me, own, gates, ups, squares, model_width):
    block, both = own.shape
    outs = [bf16(block, both // 4)] * 2
    return call(functools.partial(act_kernel, model_width), "act", outs, me, own, gates, ups, squares)


def third_kernel(me, h0, h1, t0, t1, weight, o0, o1, o2, o3, hidden):
    slots = 2 * CAP
    block, units = hidden.shape
    size = units // 4
    width = o0.shape[1]
    for index, pair in enumerate(((h0, h1), (t0, t1))):
        for place, ref in enumerate(pair):
            start = ((me[1] ^ index) * 2 + place) * size
            hidden[:, pl.ds(pl.multiple_of(start, size), size)] = ref[...]
    results = []
    for part in range(PARTS):
        columns = slice(part * width, (part + 1) * width)
        results.append(matmul(hidden[...], weight[:, columns]))
    for apart, out in enumerate((o0, o1, o2, o3)):
        rows = [result[apart * slots:(apart + 1) * slots, :] for result in results]
        out[...] = jnp.concatenate(rows, axis=0).astype(jnp.bfloat16)


def third(me, hidden, hidden_other, weight):
    block = hidden[0].shape[0]
    units, half = weight.shape
    outs = [bf16(block, half // PARTS)] * EXPERTS
    scratch = [pltpu.VMEM((block, units), jnp.bfloat16)]
    return call(third_kernel, "third", outs, me, *hidden, *hidden_other, weight, scratch=scratch)


def mixed_parts(me, table, turn, received, tokens):
    rows = tokens // 2
    width = received[0].shape[1]
    total = PARTS * tokens
    slots = 2 * CAP
    expert = me[0] ^ iota((total, 128), 1)
    chosen = table[:, 4 * turn:4 * turn + 2].astype(jnp.int32)
    share = table[:, 4 * turn + 2:4 * turn + 4]
    hits = [chosen[:, k:k + 1] == expert for k in range(2)]
    weight = jnp.where(hits[0], share[:, 0:1], 0.0) + jnp.where(hits[1], share[:, 1:2], 0.0)
    named = hits[0] | hits[1]
    earlier = (iota((total, total), 0) // rows == iota((total, total), 1) // rows) & (
        iota((total, total), 0) > iota((total, total), 1)
    )
    before = matmul(ones_where(earlier), ones_where(named))
    line = iota((total, 128), 0)
    start = line // tokens * slots + line // rows % 2 * CAP
    place = jnp.where(named, start + before.astype(jnp.int32), -1)
    mixed = jnp.zeros((total, width), jnp.float32)
    for apart, ref in enumerate(received):
        hit = iota((total, PARTS * slots), 1) == place[:, apart:apart + 1]
        spread = jnp.where(hit, weight[:, apart:apart + 1], 0.0)
        high = spread.astype(jnp.bfloat16)
        low = (spread - high.astype(jnp.float32)).astype(jnp.bfloat16)
        mixed = mixed + matmul(high, ref[...]) + matmul(low, ref[...])
    return mixed


def mix_kernel(turn, me, state, table, r0, r1, r2, r3, out):
    tokens = state.shape[0]
    width = r0.shape[1]
    mixed = mixed_parts(me, table, turn, (r0, r1, r2, r3), tokens)
    for part in range(PARTS):
        span = slice(part * width, (part + 1) * width)
        summed = state[:, span].astype(jnp.float32) + mixed[part * tokens:(part + 1) * tokens, :]
        out[:, span] = summed.astype(jnp.bfloat16)


def halves_kernel(turn, me, state, table, *refs):
    *received, upper, lower, result = refs
    mix_kernel(turn, me, state, table, *received, result)
    upper[...] = result[:upper.shape[0], :]
    lower[...] = result[upper.shape[0]:, :]


def mix(me, turn, state, table, received, after):
    kernel = functools.partial(halves_kernel, turn)
    tokens, half = state.shape
    outs = [bf16(tokens // 2, half)] * 2
    scratch = [pltpu.VMEM(state.shape, jnp.bfloat16)]
    return call(kernel, "mix", outs, me, state, table, *received, after=after, scratch=scratch)


def last_kernel(turn, me, state, table, r0, r1, r2, r3, kept, sent, result):
    rows = kept.shape[0]
    mix_kernel(turn, me, state, table, r0, r1, r2, r3, result)
    kept[...] = result[pl.ds(pl.multiple_of(me[1] * rows, rows), rows), :]
    sent[...] = result[pl.ds(pl.multiple_of((1 - me[1]) * rows, rows), rows), :]


def last(me, turn, state, table, received, after):
    tokens, half = state.shape
    outs = [bf16(tokens // 2, half)] * 2
    scratch = [pltpu.VMEM(state.shape, jnp.bfloat16)]
    return call(functools.partial(last_kernel, turn), "last", outs, me, state, table, *received, after=after, scratch=scratch)


def finish_kernel(me, kept, other, out):
    half = kept.shape[1]
    out[:, pl.ds(pl.multiple_of(me[1] * half, half), half)] = kept[...]
    out[:, pl.ds(pl.multiple_of((1 - me[1]) * half, half), half)] = other[...]


def finish(me, kept, other):
    return call(finish_kernel, "finish", bf16(kept.shape[0], 2 * kept.shape[1]), me, kept, other)


def along(block, apart):
    return lax.ppermute(block, "expert", [(i, i ^ 2 * apart) for i in range(lax.axis_size("expert"))])


def across(blocks, behind=None):
    own, near, two, three = blocks
    if behind is not None:
        two, three, *behind[2:] = lax.optimization_barrier((two, three, *behind[2:]))
        near, behind[1] = lax.optimization_barrier((near, behind[1]))
    two, three = along(two, 2), along(three, 3)
    return [own, along(near, 1), two, three]


def paired_shards(
    east_batch,
    west_batch,
    east_entering,
    west_entering,
    east_experts,
    west_experts,
    east_gates,
    west_gates,
    norm_gain,
    expert_in,
    expert_down,
):
    section_index = lax.axis_index("pipe")
    section_count = lax.axis_size("pipe")
    member = lax.axis_index("expert")
    edges = [section_index == 0, section_index == section_count - 1]
    me = jnp.stack([member // 2, member % 2, *edges]).astype(jnp.int32)
    rows, model_width = east_batch.shape[1:]
    kinds = [
        jnp.swapaxes(array[tick, 0], 0, 1).astype(jnp.float32)
        for experts, gates in ((east_experts, east_gates), (west_experts, west_gates))
        for tick in range(TICKS)
        for array in (experts, gates)
    ]
    lists = jnp.concatenate(kinds, axis=0)

    batches = [east_batch[0], west_batch[0]]
    entering = [east_entering[0], west_entering[0]]
    batches_other = [partner(cut(me, batch), "expert", 0) for batch in batches]
    as_rows, as_columns = tables(me, lists, partner(lists, "expert", 0))
    entering_other = [partner(cut(me, batch), "expert", 0) for batch in entering]
    moved = [None, None]
    results = [None, None]
    states = [None, None]
    ahead = None
    for tick in range(TICKS):
        final = tick + 1 == TICKS
        arrived = [None, None]
        for stream in range(2):
            turn = stream * TICKS + tick
            if tick == 0:
                after = []
                if stream == 1:
                    weight_in, weight_out = load(me, expert_in[0, 0], expert_down[0, 0], [states[0]])
                    after = [weight_in, *entering_other]
                sent, states[stream] = enter(me, turn, batches[stream], batches_other[stream], as_rows, after)
            else:
                sent, states[stream] = relay(
                    me, turn, stream, moved[stream], entering[stream], entering_other[stream], as_rows
                )
                if stream == 0:
                    pieces_now = mix(me, turn_before, state_before, as_columns, ahead, [sent[0]])
                    moved[1] = [shifted(piece, "pipe", -1) for piece in pieces_now]
            arrived[stream] = across(sent, ahead)
            ahead = arrived[stream]
        behind = states[1]
        for stream in range(2):
            turn = stream * TICKS + tick
            gates, ups, scaled, squares = first(me, arrived[stream], norm_gain, weight_in, [behind])
            gates, ups = partner(gates, "expert", 0), partner(ups, "expert", 0)
            own = own_half(me, scaled, weight_in)
            hidden = act(me, own, gates, ups, squares, model_width)
            result = third(me, hidden, [partner(half, "expert", 0) for half in hidden], weight_out)
            behind = result[0]
            arrived[stream] = across(result, ahead)
            ahead = arrived[stream]
        if final:
            for stream in range(2):
                turn = stream * TICKS + tick
                kept, sent = last(me, turn, states[stream], as_columns, arrived[stream], [behind])
                results[stream] = finish(me, kept, partner(sent, "expert", 0))
        else:
            pieces_now = mix(me, tick, states[0], as_columns, arrived[0], [behind])
            moved[0] = [shifted(piece, "pipe", 1) for piece in pieces_now]
            turn_before, state_before = TICKS + tick, states[1]
    return (results[0][None], results[1][None])


def solution(mesh):
    in_specs = (
        P("pipe", "expert", None),
        P("pipe", "expert", None),
        P(None, "expert", None),
        P(None, "expert", None),
        P(None, "pipe", "expert", None),
        P(None, "pipe", "expert", None),
        P(None, "pipe", "expert", None),
        P(None, "pipe", "expert", None),
        P("pipe", None),
        P("pipe", "expert", None, None),
        P("pipe", "expert", None, None),
    )
    out_specs = (P("pipe", "expert", None), P("pipe", "expert", None))
    groups = mesh.shape["expert"] // EXPERTS
    shards = paired_shards if groups == 2 else general_shards
    return jax.shard_map(shards, mesh=mesh, in_specs=in_specs, out_specs=out_specs, check_vma=False)
```

```python
import functools

import jax
import jax.numpy as jnp
from jax import lax
from jax.experimental import pallas as pl
from jax.experimental.pallas import tpu as pltpu
from jax.sharding import PartitionSpec as P

EXPERTS = 4
TICKS = 2
CAP = 18


EPSILON = 1e-06


def partner(shard, axis, apart):
    return lax.ppermute(shard, axis, [(i, i ^ 1 << apart) for i in range(lax.axis_size(axis))])


def shifted(block, axis, distance):
    devices = range(lax.axis_size(axis))
    route = [(i - distance, i) for i in devices if i - distance in devices]
    return lax.ppermute(block, axis, route)


def rms_scaled(joined_rows, gain_row):
    values = joined_rows.astype(jnp.float32)
    scale_row = lax.rsqrt(jnp.mean(values * values, axis=-1, keepdims=True) + EPSILON)
    return (values * scale_row * gain_row[None, :]).astype(jnp.bfloat16)


def slot_tables(joined_routes, joined_shares, batch_count, experts, capacity):
    total_rows = joined_routes.shape[0]
    row_count = total_rows // batch_count
    onehot = (
        joined_routes[:, :, None] == jnp.arange(experts, dtype=jnp.int32)[None, None, :]
    ).astype(jnp.int32)
    per_row = jnp.sum(onehot, axis=1).reshape(batch_count, row_count, experts)
    before = (jnp.cumsum(per_row, axis=1) - per_row).reshape(total_rows, experts)
    slot_of = jnp.sum(onehot * before[:, None, :], axis=2)
    offset = jnp.arange(total_rows, dtype=jnp.int32) // row_count * capacity
    slot_of = slot_of + offset[:, None]
    slot_ids = jnp.arange(batch_count * capacity, dtype=jnp.int32)
    slot_hit = (slot_of[:, :, None] == slot_ids[None, None, :]).astype(jnp.float32)
    onehot_float = onehot.astype(jnp.float32)
    placement = jnp.einsum("rke,rkc->ecr", onehot_float, slot_hit, precision=lax.Precision.HIGHEST)
    weighted = jnp.einsum(
        "rke,rkc->rec",
        onehot_float * joined_shares[:, :, None],
        slot_hit,
        precision=lax.Precision.HIGHEST,
    )
    return (placement, weighted)


def halving_sum(partial_value, groups, halved_bits):
    row_count = partial_value.shape[0]
    slice_width = partial_value.shape[1] // (2 * groups)
    holding = partial_value.reshape(row_count, 2, groups, slice_width)
    member_index = lax.axis_index("expert")
    held_count = groups
    for bit_index in range(halved_bits):
        own_bit = member_index >> bit_index & 1
        reshaped = holding.reshape(row_count, 2, held_count // 2, 2, slice_width)
        kept_half = lax.dynamic_index_in_dim(reshaped, own_bit, 3, keepdims=False)
        sent_half = lax.dynamic_index_in_dim(reshaped, 1 - own_bit, 3, keepdims=False)
        holding = kept_half + partner(sent_half, "expert", bit_index)
        held_count = held_count // 2
    holding = holding + partner(holding, "expert", halved_bits)
    return (holding[:, 0], holding[:, 1])


def doubling_gather(own_piece, gathered_bits):
    row_count, held_count, slice_width = own_piece.shape
    holding = own_piece
    member_index = lax.axis_index("expert")
    for bit_index in reversed(range(gathered_bits)):
        own_bit = member_index >> bit_index & 1
        arrived = partner(holding, "expert", bit_index)
        first_half = jnp.where(own_bit == 0, holding, arrived)
        second_half = jnp.where(own_bit == 0, arrived, holding)
        stacked = jnp.stack([first_half, second_half], axis=2)
        holding = stacked.reshape(row_count, -1, slice_width)
    return holding.reshape(row_count, -1)


def expert_layer(batch_list, route_list, share_list, gain_row, weight_in, weight_out):
    batch_count = len(batch_list)
    row_count = batch_list[0].shape[0]
    model_width = batch_list[0].shape[1]
    groups = lax.axis_size("expert") // EXPERTS
    bit_count = groups.bit_length() - 1
    halved_bits = bit_count - 1
    feat_width = model_width // groups
    joined_rows = batch_list[0]
    joined_routes = route_list[0]
    joined_shares = share_list[0]
    normed = rms_scaled(joined_rows, gain_row)
    placement, weighted = slot_tables(joined_routes, joined_shares, batch_count, EXPERTS, CAP)
    total_rows = batch_count * row_count
    normed_split = normed.reshape(total_rows, groups, feat_width)
    outgoing = jnp.einsum(
        "ecr,rwf->ewcf",
        placement.astype(jnp.bfloat16),
        normed_split,
        preferred_element_type=jnp.float32,
    ).astype(jnp.bfloat16)
    outgoing = outgoing.reshape(EXPERTS * groups, batch_count * CAP, feat_width)
    arrived = lax.all_to_all(outgoing, "expert", split_axis=0, concat_axis=0, tiled=True)
    sources, slot_count, block_width = arrived.shape
    flat_rows = arrived.reshape(sources * slot_count, block_width)
    partial_value = jnp.dot(flat_rows, weight_in, preferred_element_type=jnp.float32)
    gate_part, up_part = halving_sum(partial_value, groups, halved_bits)
    own_piece = (jax.nn.silu(gate_part) * up_part).astype(jnp.bfloat16)
    hidden = doubling_gather(own_piece, halved_bits)
    result = jnp.dot(hidden, weight_out, preferred_element_type=jnp.float32).astype(jnp.bfloat16)
    returned = lax.all_to_all(
        result.reshape(sources, slot_count, block_width),
        "expert",
        split_axis=0,
        concat_axis=0,
        tiled=True,
    )
    returned_split = returned.reshape(EXPERTS, groups, batch_count * CAP, feat_width).astype(
        jnp.float32
    )
    mixed = jnp.einsum(
        "rec,ewcf->rwf", weighted, returned_split, precision=lax.Precision.HIGHEST
    ).reshape(total_rows, model_width)
    output = (joined_rows.astype(jnp.float32) + mixed).astype(jnp.bfloat16)
    return [output]


def general_shards(
    east_batch,
    west_batch,
    east_entering,
    west_entering,
    east_experts,
    west_experts,
    east_gates,
    west_gates,
    norm_gain,
    expert_in,
    expert_down,
):
    section_index = lax.axis_index("pipe")
    section_count = lax.axis_size("pipe")
    gain_row = norm_gain[0]
    weight_in = expert_in[0, 0]
    weight_out = expert_down[0, 0]
    east_now = east_batch[0]
    west_now = west_batch[0]
    for tick_index in range(TICKS):
        east_routes = east_experts[tick_index, 0]
        west_routes = west_experts[tick_index, 0]
        east_shares = east_gates[tick_index, 0]
        west_shares = west_gates[tick_index, 0]
        east_now = expert_layer(
            [east_now], [east_routes], [east_shares], gain_row, weight_in, weight_out
        )[0]
        west_now = expert_layer(
            [west_now], [west_routes], [west_shares], gain_row, weight_in, weight_out
        )[0]
        if tick_index + 1 < TICKS:
            moved_east = shifted(east_now, "pipe", 1)
            east_now = jnp.where(section_index == 0, east_entering[tick_index], moved_east)
            moved_west = shifted(west_now, "pipe", -1)
            west_now = jnp.where(
                section_index == section_count - 1, west_entering[tick_index], moved_west
            )
    return (east_now[None], west_now[None])


PARTS = 4
LIMIT = 16 * 2**20


def whole(count):
    return [pl.BlockSpec(memory_space=pltpu.VMEM)] * count


def without(kernel, place, count, *refs):
    kernel(*refs[:place], *refs[place + count:])


def call(kernel, name, out_shape, me, *arrays, after=(), scratch=(), limit=LIMIT):
    several = isinstance(out_shape, list)
    if after:
        kernel = functools.partial(without, kernel, 1 + len(arrays), len(after))
    unread = [pl.BlockSpec(memory_space=pl.ANY)] * len(after)
    return pl.pallas_call(
        kernel,
        out_shape=out_shape,
        in_specs=[pl.BlockSpec(memory_space=pltpu.SMEM)] + whole(len(arrays)) + unread,
        out_specs=whole(len(out_shape)) if several else whole(1)[0],
        scratch_shapes=list(scratch),
        compiler_params=pltpu.CompilerParams(vmem_limit_bytes=limit),
        cost_estimate=pl.CostEstimate(flops=0, bytes_accessed=0, transcendentals=0),
        name=name,
    )(me, *arrays, *after)


def bf16(*shape):
    return jax.ShapeDtypeStruct(shape, jnp.bfloat16)


def f32(*shape):
    return jax.ShapeDtypeStruct(shape, jnp.float32)


def iota(shape, axis):
    return lax.broadcasted_iota(jnp.int32, shape, axis)


def matmul(a, b):
    return jnp.dot(a, b, preferred_element_type=jnp.float32)


def ones_where(condition):
    return condition.astype(jnp.float32).astype(jnp.bfloat16)


def pieces(values):
    high = values.astype(jnp.bfloat16)
    rest = values - high.astype(jnp.float32)
    middle = rest.astype(jnp.bfloat16)
    return high, middle, (rest - middle.astype(jnp.float32)).astype(jnp.bfloat16)


def cut_kernel(me, batch, kept, sent):
    half = sent.shape[1]
    kept[...] = batch[:, pl.ds(pl.multiple_of(me[1] * half, half), half)]
    sent[...] = batch[:, pl.ds(pl.multiple_of((1 - me[1]) * half, half), half)]


def cut(me, batch, after=()):
    rows, model_width = batch.shape
    return call(cut_kernel, "cut", [bf16(rows, model_width // 2)] * 2, me, batch, after=after)


def crossed(halves):
    return halves[0], partner(halves[1], "expert", 0)


def tables_kernel(me, own, other, as_rows, as_columns):
    rows = own.shape[1]
    total = as_rows.shape[1]
    row_sum = jnp.zeros(as_rows.shape, jnp.float32)
    column_sum = jnp.zeros(as_columns.shape, jnp.float32)
    for source, x in ((own, me[1]), (other, 1 - me[1])):
        token, column = iota((rows, total), 0), iota((rows, total), 1)
        spread = ones_where((column % rows == token) & (column // rows % 2 == x))
        line, lane = iota((total, rows), 0), iota((total, rows), 1)
        gather = ones_where((line % rows == lane) & (line // rows % 2 == x))
        high, middle, low = pieces(source[...])
        row_sum = row_sum + ((matmul(low, spread) + matmul(middle, spread)) + matmul(high, spread))
        turned = [
            lax.dot_general(gather, piece, (((1,), (1,)), ((), ())), preferred_element_type=jnp.float32)
            for piece in (low, middle, high)
        ]
        column_sum = column_sum + ((turned[0] + turned[1]) + turned[2])
    as_rows[...] = row_sum
    as_columns[...] = column_sum


def tables(me, own, other):
    kinds, rows = own.shape
    total = 2 * PARTS * rows
    return call(tables_kernel, "tables", [f32(kinds, total), f32(total, kinds)], me, own, other)


def joined(me, kept, other, state):
    rows = kept.shape[0]
    state[pl.ds(pl.multiple_of(me[1] * rows, rows), rows), :] = kept[...]
    state[pl.ds(pl.multiple_of((1 - me[1]) * rows, rows), rows), :] = other[...]


def packed(me, state, table, turn, outs, stacked):
    tokens, half = state.shape
    rows = tokens // 2
    width = half // PARTS
    total = PARTS * tokens
    slots = 2 * CAP
    for part in range(PARTS):
        stacked[part * tokens:(part + 1) * tokens, :] = state[:, part * width:(part + 1) * width]
    expert = me[0] ^ iota((8, total), 0)
    chosen = table[4 * turn:4 * turn + 2, :].astype(jnp.int32)
    named = (chosen[0:1, :] == expert) | (chosen[1:2, :] == expert)
    earlier = (iota((total, total), 0) // rows == iota((total, total), 1) // rows) & (
        iota((total, total), 0) < iota((total, total), 1)
    )
    before = matmul(ones_where(named), ones_where(earlier))
    column = iota((8, total), 1)
    start = column // tokens * slots + column // rows % 2 * CAP
    place = jnp.where(named, start + before.astype(jnp.int32), -1)
    for apart in range(EXPERTS):
        hit = iota((PARTS * slots, total), 0) == place[apart:apart + 1, :]
        outs[apart][...] = matmul(ones_where(hit), stacked[...]).astype(jnp.bfloat16)


def enter_kernel(turn, me, kept, other, table, o0, o1, o2, o3, state, stacked):
    joined(me, kept, other, state)
    packed(me, state, table, turn, (o0, o1, o2, o3), stacked)


def relay_kernel(turn, edge, me, moved, moved_rest, kept, other, table, o0, o1, o2, o3, state, stacked):
    state[:moved.shape[0], :] = moved[...]
    state[moved.shape[0]:, :] = moved_rest[...]

    @pl.when(me[2 + edge] == 1)
    def _():
        joined(me, kept, other, state)

    packed(me, state, table, turn, (o0, o1, o2, o3), stacked)


def pack_shapes(rows, half):
    width = half // PARTS
    outs = [bf16(PARTS * 2 * CAP, width)] * EXPERTS + [bf16(2 * rows, half)]
    return outs, [pltpu.VMEM((PARTS * 2 * rows, width), jnp.bfloat16)]


def enter(me, turn, kept, other, table, after):
    outs, scratch = pack_shapes(*other.shape)
    made = call(functools.partial(enter_kernel, turn), "enter", outs, me, kept, other, table, after=after, scratch=scratch)
    return made[:EXPERTS], made[EXPERTS]


def relay(me, turn, edge, moved, kept, other, table):
    outs, scratch = pack_shapes(*other.shape)
    kernel = functools.partial(relay_kernel, turn, edge)
    made = call(kernel, "relay", outs, me, *moved, kept, other, table, scratch=scratch)
    return made[:EXPERTS], made[EXPERTS]


def load_kernel(me, source, other_source, out, other_out, done):
    copies = [
        pltpu.make_async_copy(source, out, done.at[0]),
        pltpu.make_async_copy(other_source, other_out, done.at[1]),
    ]
    for copy in copies:
        copy.start()
    for copy in copies:
        copy.wait()


def load(me, weight, other_weight, after):
    arrays = [weight, other_weight]
    kernel = functools.partial(without, load_kernel, 3, len(after))
    return pl.pallas_call(
        kernel,
        out_shape=[bf16(*array.shape) for array in arrays],
        in_specs=[pl.BlockSpec(memory_space=pltpu.SMEM)] + [pl.BlockSpec(memory_space=pltpu.HBM)] * 2
        + [pl.BlockSpec(memory_space=pl.ANY)] * len(after),
        out_specs=whole(2),
        scratch_shapes=[pltpu.SemaphoreType.DMA((2,))],
        compiler_params=pltpu.CompilerParams(vmem_limit_bytes=LIMIT),
        cost_estimate=pl.CostEstimate(flops=0, bytes_accessed=0, transcendentals=0),
        name="load",
    )(me, *arrays, *after)


def first_kernel(me, r0, r1, r2, r3, gain, weight, gates, ups, rows_out, squares):
    slots = 2 * CAP
    block, width = r0.shape
    units = weight.shape[1] // 4
    held = [ref[...].astype(jnp.float32) for ref in (r0, r1, r2, r3)]
    total = jnp.zeros((block, 1), jnp.float32)
    for part in range(PARTS):
        values = jnp.concatenate([rows[part * slots:(part + 1) * slots, :] for rows in held], axis=0)
        total = total + jnp.sum(values * values, axis=1, keepdims=True)
        start = pl.multiple_of(me[1] * PARTS * width + part * width, width)
        scaled = values * gain[:, pl.ds(start, width)]
        rows_out[:, part * width:(part + 1) * width] = scaled.astype(jnp.bfloat16)
    squares[...] = jnp.broadcast_to(total, squares.shape)
    lane = iota(squares.shape, 1)
    high, middle, low = [piece.astype(jnp.float32) for piece in pieces(total)]
    sent = jnp.where(lane == 0, high, jnp.where(lane == 1, middle, jnp.where(lane == 2, low, 0.0)))
    turned = lax.dot_general(
        sent.astype(jnp.bfloat16),
        ones_where(iota((block, block), 0) == iota((block, block), 1)),
        (((0,), (0,)), ((), ())),
        preferred_element_type=jnp.float32,
    )
    extra = gates.shape[0] - block
    gates[block:, :] = jnp.zeros((extra, units), jnp.bfloat16)
    gates[block:, :block] = turned[:extra, :].astype(jnp.bfloat16)
    for kind in range(2):
        start = pl.multiple_of(units * (2 * kind + 1 - me[1]), units)
        columns = matmul(rows_out[...], weight[:, pl.ds(start, units)]).astype(jnp.bfloat16)
        (gates, ups)[kind][:block, :] = columns


def first(me, received, gain, weight, after):
    block, width = received[0].shape
    half, both = weight.shape
    outs = [bf16(block + 16, both // 4), bf16(block, both // 4), bf16(block, half), f32(block, 128)]
    return call(first_kernel, "first", outs, me, *received, gain, weight, after=after)


def own_kernel(me, rows_in, weight, own):
    units = weight.shape[1] // 4
    for kind in range(2):
        start = pl.multiple_of(units * (2 * kind + me[1]), units)
        own[:, kind * units:(kind + 1) * units] = matmul(rows_in[...], weight[:, pl.ds(start, units)])


def own_half(me, rows_in, weight):
    return call(own_kernel, "own", f32(rows_in.shape[0], weight.shape[1] // 2), me, rows_in, weight)


def act_kernel(model_width, me, own, gates, ups, squares, h0, h1):
    block, both = own.shape
    units = both // 2
    pair = lax.dot_general(
        ones_where(iota((block, block), 0) == iota((block, block), 1)),
        gates[block:, :block],
        (((1,), (1,)), ((), ())),
        preferred_element_type=jnp.float32,
    )
    mean = (squares[:, 0:1] + ((pair[:, 2:3] + pair[:, 1:2]) + pair[:, 0:1])) / model_width
    scale = lax.rsqrt(mean + EPSILON)
    gate = (own[:, :units] + gates[:block, :].astype(jnp.float32)) * scale
    up = (own[:, units:] + ups[...].astype(jnp.float32)) * scale
    hidden = (gate / (1.0 + jnp.exp(-gate)) * up).astype(jnp.bfloat16)
    h0[...] = hidden[:, :units // 2]
    h1[...] = hidden[:, units // 2:]


def act(me, own, gates, ups, squares, model_width):
    block, both = own.shape
    outs = [bf16(block, both // 4)] * 2
    return call(functools.partial(act_kernel, model_width), "act", outs, me, own, gates, ups, squares)


def third_kernel(me, h0, h1, t0, t1, weight, o0, o1, o2, o3, hidden):
    slots = 2 * CAP
    block, units = hidden.shape
    size = units // 4
    width = o0.shape[1]
    for index, pair in enumerate(((h0, h1), (t0, t1))):
        for place, ref in enumerate(pair):
            start = ((me[1] ^ index) * 2 + place) * size
            hidden[:, pl.ds(pl.multiple_of(start, size), size)] = ref[...]
    results = []
    for part in range(PARTS):
        columns = slice(part * width, (part + 1) * width)
        results.append(matmul(hidden[...], weight[:, columns]))
    for apart, out in enumerate((o0, o1, o2, o3)):
        rows = [result[apart * slots:(apart + 1) * slots, :] for result in results]
        out[...] = jnp.concatenate(rows, axis=0).astype(jnp.bfloat16)


def third(me, hidden, hidden_other, weight):
    block = hidden[0].shape[0]
    units, half = weight.shape
    outs = [bf16(block, half // PARTS)] * EXPERTS
    scratch = [pltpu.VMEM((block, units), jnp.bfloat16)]
    return call(third_kernel, "third", outs, me, *hidden, *hidden_other, weight, scratch=scratch)


def spread_gates(me, table, turn, rows, start):
    total = table.shape[0]
    slots = 2 * CAP
    expert = me[0] ^ iota((total, 128), 1)
    chosen = table[:, 4 * turn:4 * turn + 2].astype(jnp.int32)
    share = table[:, 4 * turn + 2:4 * turn + 4]
    hits = [chosen[:, k:k + 1] == expert for k in range(2)]
    weight = jnp.where(hits[0], share[:, 0:1], 0.0) + jnp.where(hits[1], share[:, 1:2], 0.0)
    named = hits[0] | hits[1]
    earlier = (iota((total, total), 0) // rows == iota((total, total), 1) // rows) & (
        iota((total, total), 0) > iota((total, total), 1)
    )
    before = matmul(ones_where(earlier), ones_where(named))
    place = jnp.where(named, start + before.astype(jnp.int32), -1)
    spreads = []
    for apart in range(EXPERTS):
        hit = iota((total, PARTS * slots), 1) == place[:, apart:apart + 1]
        spreads.append(jnp.where(hit, weight[:, apart:apart + 1], 0.0))
    return spreads


def combined(spreads, received):
    mixed = jnp.zeros((spreads[0].shape[0], received[0].shape[1]), jnp.float32)
    for spread, ref in zip(spreads, received):
        high = spread.astype(jnp.bfloat16)
        low = (spread - high.astype(jnp.float32)).astype(jnp.bfloat16)
        mixed = mixed + matmul(high, ref[...]) + matmul(low, ref[...])
    return mixed


def mixed_parts(me, table, turn, received, tokens):
    rows = tokens // 2
    line = iota((PARTS * tokens, 128), 0)
    start = line // tokens * 2 * CAP + line // rows % 2 * CAP
    return combined(spread_gates(me, table, turn, rows, start), received)


def mix_kernel(turn, me, state, table, r0, r1, r2, r3, out):
    tokens = state.shape[0]
    width = r0.shape[1]
    mixed = mixed_parts(me, table, turn, (r0, r1, r2, r3), tokens)
    for part in range(PARTS):
        span = slice(part * width, (part + 1) * width)
        summed = state[:, span].astype(jnp.float32) + mixed[part * tokens:(part + 1) * tokens, :]
        out[:, span] = summed.astype(jnp.bfloat16)


def halves_kernel(turn, me, state, table, *refs):
    *received, upper, lower, result = refs
    mix_kernel(turn, me, state, table, *received, result)
    upper[...] = result[:upper.shape[0], :]
    lower[...] = result[upper.shape[0]:, :]


def mix(me, turn, state, table, received, after):
    kernel = functools.partial(halves_kernel, turn)
    tokens, half = state.shape
    outs = [bf16(tokens // 2, half)] * 2
    scratch = [pltpu.VMEM(state.shape, jnp.bfloat16)]
    return call(kernel, "mix", outs, me, state, table, *received, after=after, scratch=scratch)


def last_kernel(turn, side, me, state, table, r0, r1, r2, r3, out, lines):
    rows, half = out.shape
    width = r0.shape[1]
    slots = 2 * CAP
    total = PARTS * rows
    source = me[1] ^ side
    for part in range(PARTS):
        start = pl.multiple_of((2 * part + source) * rows, rows)
        lines[part * rows:(part + 1) * rows, :] = table[pl.ds(start, rows), :]
    spreads = spread_gates(me, lines, turn, rows, iota((total, 128), 0) // rows * slots + source * CAP)
    mixed = combined(spreads, (r0, r1, r2, r3))
    start = pl.multiple_of(source * rows, rows)
    for part in range(PARTS):
        span = slice(part * width, (part + 1) * width)
        values = state[pl.ds(start, rows), span].astype(jnp.float32)
        out[:, span] = (values + mixed[part * rows:(part + 1) * rows, :]).astype(jnp.bfloat16)


def last(me, turn, side, state, table, received, after):
    tokens, half = state.shape
    rows = tokens // 2
    scratch = [pltpu.VMEM((PARTS * rows, table.shape[1]), jnp.float32)]
    kernel = functools.partial(last_kernel, turn, side)
    return call(kernel, "last", bf16(rows, half), me, state, table, *received, after=after, scratch=scratch)


def finish_kernel(me, kept, other, out):
    half = kept.shape[1]
    out[:, pl.ds(pl.multiple_of(me[1] * half, half), half)] = kept[...]
    out[:, pl.ds(pl.multiple_of((1 - me[1]) * half, half), half)] = other[...]


def finish(me, kept, other):
    return call(finish_kernel, "finish", bf16(kept.shape[0], 2 * kept.shape[1]), me, kept, other)


def along(block, apart):
    return lax.ppermute(block, "expert", [(i, i ^ 2 * apart) for i in range(lax.axis_size("expert"))])


def across(blocks, behind=None, hold=False):
    own, near, two, three = blocks
    if behind is not None:
        two, three, *behind[2:] = lax.optimization_barrier((two, three, *behind[2:]))
        near, behind[1] = lax.optimization_barrier((near, behind[1]))
    return [own, along(near, 1), along(two, 2), three if hold else along(three, 3)]


def paired_shards(
    east_batch,
    west_batch,
    east_entering,
    west_entering,
    east_experts,
    west_experts,
    east_gates,
    west_gates,
    norm_gain,
    expert_in,
    expert_down,
):
    section_index = lax.axis_index("pipe")
    section_count = lax.axis_size("pipe")
    member = lax.axis_index("expert")
    edges = [section_index == 0, section_index == section_count - 1]
    me = jnp.stack([member // 2, member % 2, *edges]).astype(jnp.int32)
    rows, model_width = east_batch.shape[1:]
    kinds = [
        jnp.swapaxes(array[tick, 0], 0, 1).astype(jnp.float32)
        for experts, gates in ((east_experts, east_gates), (west_experts, west_gates))
        for tick in range(TICKS)
        for array in (experts, gates)
    ]
    lists = jnp.concatenate(kinds, axis=0)

    batches = [east_batch[0], west_batch[0]]
    entering = [east_entering[0], west_entering[0]]
    east_halves = cut(me, batches[0])
    as_rows, as_columns = tables(me, lists, partner(lists, "expert", 0))
    east_halves = crossed(east_halves)
    moved = [None, None]
    results = [None, None]
    states = [None, None]
    ahead = None
    for tick in range(TICKS):
        final = tick + 1 == TICKS
        arrived = [None, None]
        for stream in range(2):
            turn = stream * TICKS + tick
            if tick == 0:
                after, west_halves = [], None
                if stream == 1:
                    west_halves = crossed(cut(me, batches[1], [states[0]]))
                    entering_halves = [crossed(cut(me, batch, [states[0]])) for batch in entering]
                    weight_in, weight_out = load(me, expert_in[0, 0], expert_down[0, 0], [states[0]])
                    after = [weight_in]
                sent, states[stream] = enter(me, turn, *(east_halves, west_halves)[stream], as_rows, after)
            else:
                sent, states[stream] = relay(
                    me, turn, stream, moved[stream], *entering_halves[stream], as_rows
                )
                if stream == 0:
                    pieces_now = mix(me, turn_before, state_before, as_columns, ahead, [sent[0]])
                    moved[1] = [shifted(piece, "pipe", -1) for piece in pieces_now]
            arrived[stream] = across(sent, ahead, stream == 1)
            ahead = arrived[stream]
        behind = states[1]
        crossings = [halves[1] for halves in entering_halves] if tick == 0 else []
        for stream in range(2):
            turn = stream * TICKS + tick
            gates, ups, scaled, squares = first(me, arrived[stream], norm_gain, weight_in, [behind, *crossings])
            crossings = []
            held = arrived[1 - stream]
            scaled, held[3] = lax.optimization_barrier((scaled, held[3]))
            held[3] = along(held[3], 3)
            gates, ups = partner(gates, "expert", 0), partner(ups, "expert", 0)
            own = own_half(me, scaled, weight_in)
            hidden = act(me, own, gates, ups, squares, model_width)
            result = third(me, hidden, [partner(half, "expert", 0) for half in hidden], weight_out)
            behind = result[0]
            arrived[stream] = across(result, ahead, stream == 0)
            ahead = arrived[stream]
        if final:
            for stream in range(2):
                turn = stream * TICKS + tick
                sent = last(me, turn, 1, states[stream], as_columns, arrived[stream], [behind])
                other = partner(sent, "expert", 0)
                kept = last(me, turn, 0, states[stream], as_columns, arrived[stream], [sent])
                results[stream] = finish(me, kept, other)
        else:
            pieces_now = mix(me, tick, states[0], as_columns, arrived[0], [behind])
            moved[0] = [shifted(piece, "pipe", 1) for piece in pieces_now]
            turn_before, state_before = TICKS + tick, states[1]
    return (results[0][None], results[1][None])


def solution(mesh):
    in_specs = (
        P("pipe", "expert", None),
        P("pipe", "expert", None),
        P(None, "expert", None),
        P(None, "expert", None),
        P(None, "pipe", "expert", None),
        P(None, "pipe", "expert", None),
        P(None, "pipe", "expert", None),
        P(None, "pipe", "expert", None),
        P("pipe", None),
        P("pipe", "expert", None, None),
        P("pipe", "expert", None, None),
    )
    out_specs = (P("pipe", "expert", None), P("pipe", "expert", None))
    groups = mesh.shape["expert"] // EXPERTS
    shards = paired_shards if groups == 2 else general_shards
    return jax.shard_map(shards, mesh=mesh, in_specs=in_specs, out_specs=out_specs, check_vma=False)
```

```python
import functools

import jax
import jax.numpy as jnp
from jax import lax
from jax.experimental import pallas as pl
from jax.experimental.pallas import tpu as pltpu
from jax.sharding import PartitionSpec as P

EXPERTS = 4
TICKS = 2
CAP = 18


EPSILON = 1e-06


def partner(shard, axis, apart):
    return lax.ppermute(shard, axis, [(i, i ^ 1 << apart) for i in range(lax.axis_size(axis))])


def shifted(block, axis, distance):
    devices = range(lax.axis_size(axis))
    route = [(i - distance, i) for i in devices if i - distance in devices]
    return lax.ppermute(block, axis, route)


def rms_scaled(joined_rows, gain_row):
    values = joined_rows.astype(jnp.float32)
    scale_row = lax.rsqrt(jnp.mean(values * values, axis=-1, keepdims=True) + EPSILON)
    return (values * scale_row * gain_row[None, :]).astype(jnp.bfloat16)


def slot_tables(joined_routes, joined_shares, batch_count, experts, capacity):
    total_rows = joined_routes.shape[0]
    row_count = total_rows // batch_count
    onehot = (
        joined_routes[:, :, None] == jnp.arange(experts, dtype=jnp.int32)[None, None, :]
    ).astype(jnp.int32)
    per_row = jnp.sum(onehot, axis=1).reshape(batch_count, row_count, experts)
    before = (jnp.cumsum(per_row, axis=1) - per_row).reshape(total_rows, experts)
    slot_of = jnp.sum(onehot * before[:, None, :], axis=2)
    offset = jnp.arange(total_rows, dtype=jnp.int32) // row_count * capacity
    slot_of = slot_of + offset[:, None]
    slot_ids = jnp.arange(batch_count * capacity, dtype=jnp.int32)
    slot_hit = (slot_of[:, :, None] == slot_ids[None, None, :]).astype(jnp.float32)
    onehot_float = onehot.astype(jnp.float32)
    placement = jnp.einsum("rke,rkc->ecr", onehot_float, slot_hit, precision=lax.Precision.HIGHEST)
    weighted = jnp.einsum(
        "rke,rkc->rec",
        onehot_float * joined_shares[:, :, None],
        slot_hit,
        precision=lax.Precision.HIGHEST,
    )
    return (placement, weighted)


def halving_sum(partial_value, groups, halved_bits):
    row_count = partial_value.shape[0]
    slice_width = partial_value.shape[1] // (2 * groups)
    holding = partial_value.reshape(row_count, 2, groups, slice_width)
    member_index = lax.axis_index("expert")
    held_count = groups
    for bit_index in range(halved_bits):
        own_bit = member_index >> bit_index & 1
        reshaped = holding.reshape(row_count, 2, held_count // 2, 2, slice_width)
        kept_half = lax.dynamic_index_in_dim(reshaped, own_bit, 3, keepdims=False)
        sent_half = lax.dynamic_index_in_dim(reshaped, 1 - own_bit, 3, keepdims=False)
        holding = kept_half + partner(sent_half, "expert", bit_index)
        held_count = held_count // 2
    holding = holding + partner(holding, "expert", halved_bits)
    return (holding[:, 0], holding[:, 1])


def doubling_gather(own_piece, gathered_bits):
    row_count, held_count, slice_width = own_piece.shape
    holding = own_piece
    member_index = lax.axis_index("expert")
    for bit_index in reversed(range(gathered_bits)):
        own_bit = member_index >> bit_index & 1
        arrived = partner(holding, "expert", bit_index)
        first_half = jnp.where(own_bit == 0, holding, arrived)
        second_half = jnp.where(own_bit == 0, arrived, holding)
        stacked = jnp.stack([first_half, second_half], axis=2)
        holding = stacked.reshape(row_count, -1, slice_width)
    return holding.reshape(row_count, -1)


def expert_layer(batch_list, route_list, share_list, gain_row, weight_in, weight_out):
    batch_count = len(batch_list)
    row_count = batch_list[0].shape[0]
    model_width = batch_list[0].shape[1]
    groups = lax.axis_size("expert") // EXPERTS
    bit_count = groups.bit_length() - 1
    halved_bits = bit_count - 1
    feat_width = model_width // groups
    joined_rows = batch_list[0]
    joined_routes = route_list[0]
    joined_shares = share_list[0]
    normed = rms_scaled(joined_rows, gain_row)
    placement, weighted = slot_tables(joined_routes, joined_shares, batch_count, EXPERTS, CAP)
    total_rows = batch_count * row_count
    normed_split = normed.reshape(total_rows, groups, feat_width)
    outgoing = jnp.einsum(
        "ecr,rwf->ewcf",
        placement.astype(jnp.bfloat16),
        normed_split,
        preferred_element_type=jnp.float32,
    ).astype(jnp.bfloat16)
    outgoing = outgoing.reshape(EXPERTS * groups, batch_count * CAP, feat_width)
    arrived = lax.all_to_all(outgoing, "expert", split_axis=0, concat_axis=0, tiled=True)
    sources, slot_count, block_width = arrived.shape
    flat_rows = arrived.reshape(sources * slot_count, block_width)
    partial_value = jnp.dot(flat_rows, weight_in, preferred_element_type=jnp.float32)
    gate_part, up_part = halving_sum(partial_value, groups, halved_bits)
    own_piece = (jax.nn.silu(gate_part) * up_part).astype(jnp.bfloat16)
    hidden = doubling_gather(own_piece, halved_bits)
    result = jnp.dot(hidden, weight_out, preferred_element_type=jnp.float32).astype(jnp.bfloat16)
    returned = lax.all_to_all(
        result.reshape(sources, slot_count, block_width),
        "expert",
        split_axis=0,
        concat_axis=0,
        tiled=True,
    )
    returned_split = returned.reshape(EXPERTS, groups, batch_count * CAP, feat_width).astype(
        jnp.float32
    )
    mixed = jnp.einsum(
        "rec,ewcf->rwf", weighted, returned_split, precision=lax.Precision.HIGHEST
    ).reshape(total_rows, model_width)
    output = (joined_rows.astype(jnp.float32) + mixed).astype(jnp.bfloat16)
    return [output]


def general_shards(
    east_batch,
    west_batch,
    east_entering,
    west_entering,
    east_experts,
    west_experts,
    east_gates,
    west_gates,
    norm_gain,
    expert_in,
    expert_down,
):
    section_index = lax.axis_index("pipe")
    section_count = lax.axis_size("pipe")
    gain_row = norm_gain[0]
    weight_in = expert_in[0, 0]
    weight_out = expert_down[0, 0]
    east_now = east_batch[0]
    west_now = west_batch[0]
    for tick_index in range(TICKS):
        east_routes = east_experts[tick_index, 0]
        west_routes = west_experts[tick_index, 0]
        east_shares = east_gates[tick_index, 0]
        west_shares = west_gates[tick_index, 0]
        east_now = expert_layer(
            [east_now], [east_routes], [east_shares], gain_row, weight_in, weight_out
        )[0]
        west_now = expert_layer(
            [west_now], [west_routes], [west_shares], gain_row, weight_in, weight_out
        )[0]
        if tick_index + 1 < TICKS:
            moved_east = shifted(east_now, "pipe", 1)
            east_now = jnp.where(section_index == 0, east_entering[tick_index], moved_east)
            moved_west = shifted(west_now, "pipe", -1)
            west_now = jnp.where(
                section_index == section_count - 1, west_entering[tick_index], moved_west
            )
    return (east_now[None], west_now[None])


PARTS = 4
LIMIT = 16 * 2**20


def whole(count):
    return [pl.BlockSpec(memory_space=pltpu.VMEM)] * count


def without(kernel, place, count, *refs):
    kernel(*refs[:place], *refs[place + count:])


def call(kernel, name, out_shape, me, *arrays, after=(), scratch=(), limit=LIMIT):
    several = isinstance(out_shape, list)
    if after:
        kernel = functools.partial(without, kernel, 1 + len(arrays), len(after))
    unread = [pl.BlockSpec(memory_space=pl.ANY)] * len(after)
    return pl.pallas_call(
        kernel,
        out_shape=out_shape,
        in_specs=[pl.BlockSpec(memory_space=pltpu.SMEM)] + whole(len(arrays)) + unread,
        out_specs=whole(len(out_shape)) if several else whole(1)[0],
        scratch_shapes=list(scratch),
        compiler_params=pltpu.CompilerParams(vmem_limit_bytes=limit),
        cost_estimate=pl.CostEstimate(flops=0, bytes_accessed=0, transcendentals=0),
        name=name,
    )(me, *arrays, *after)


def bf16(*shape):
    return jax.ShapeDtypeStruct(shape, jnp.bfloat16)


def f32(*shape):
    return jax.ShapeDtypeStruct(shape, jnp.float32)


def iota(shape, axis):
    return lax.broadcasted_iota(jnp.int32, shape, axis)


def matmul(a, b):
    return jnp.dot(a, b, preferred_element_type=jnp.float32)


def ones_where(condition):
    return condition.astype(jnp.float32).astype(jnp.bfloat16)


def pieces(values):
    high = values.astype(jnp.bfloat16)
    rest = values - high.astype(jnp.float32)
    middle = rest.astype(jnp.bfloat16)
    return high, middle, (rest - middle.astype(jnp.float32)).astype(jnp.bfloat16)


def cut_kernel(count, me, *refs):
    batches, outs, done = refs[:count], refs[count:-1], refs[-1]
    half = outs[0].shape[1]
    copies = []
    for index, batch in enumerate(batches):
        for side in range(2):
            start = pl.multiple_of((me[1] ^ side) * half, half)
            place = 2 * index + side
            copies.append(pltpu.make_async_copy(batch.at[:, pl.ds(start, half)], outs[place], done.at[place]))
    for copy in copies:
        copy.start()
    for copy in copies:
        copy.wait()


def cut(me, batches, after=()):
    count = len(batches)
    rows, model_width = batches[0].shape
    kernel = functools.partial(cut_kernel, count)
    if after:
        kernel = functools.partial(without, kernel, 1 + count, len(after))
    made = pl.pallas_call(
        kernel,
        out_shape=[bf16(rows, model_width // 2)] * (2 * count),
        in_specs=[pl.BlockSpec(memory_space=pltpu.SMEM)]
        + [pl.BlockSpec(memory_space=pltpu.HBM)] * count
        + [pl.BlockSpec(memory_space=pl.ANY)] * len(after),
        out_specs=whole(2 * count),
        scratch_shapes=[pltpu.SemaphoreType.DMA((2 * count,))],
        compiler_params=pltpu.CompilerParams(vmem_limit_bytes=LIMIT),
        cost_estimate=pl.CostEstimate(flops=0, bytes_accessed=0, transcendentals=0),
        name="cut",
    )(me, *batches, *after)
    return [made[2 * index:2 * index + 2] for index in range(count)]


def crossed(halves):
    return halves[0], partner(halves[1], "expert", 0)


def tables_kernel(me, own, other, as_rows, as_columns):
    rows = own.shape[1]
    total = as_rows.shape[1]
    row_sum = jnp.zeros(as_rows.shape, jnp.float32)
    column_sum = jnp.zeros(as_columns.shape, jnp.float32)
    for source, x in ((own, me[1]), (other, 1 - me[1])):
        token, column = iota((rows, total), 0), iota((rows, total), 1)
        spread = ones_where((column % rows == token) & (column // rows % 2 == x))
        line, lane = iota((total, rows), 0), iota((total, rows), 1)
        gather = ones_where((line % rows == lane) & (line // rows % 2 == x))
        high, middle, low = pieces(source[...])
        row_sum = row_sum + ((matmul(low, spread) + matmul(middle, spread)) + matmul(high, spread))
        turned = [
            lax.dot_general(gather, piece, (((1,), (1,)), ((), ())), preferred_element_type=jnp.float32)
            for piece in (low, middle, high)
        ]
        column_sum = column_sum + ((turned[0] + turned[1]) + turned[2])
    as_rows[...] = row_sum
    as_columns[...] = column_sum


def tables(me, own, other):
    kinds, rows = own.shape
    total = 2 * PARTS * rows
    return call(tables_kernel, "tables", [f32(kinds, total), f32(total, kinds)], me, own, other)


def joined(me, kept, other, state):
    rows = kept.shape[0]
    state[pl.ds(pl.multiple_of(me[1] * rows, rows), rows), :] = kept[...]
    state[pl.ds(pl.multiple_of((1 - me[1]) * rows, rows), rows), :] = other[...]


def packed(me, state, table, turn, outs, stacked):
    tokens, half = state.shape
    rows = tokens // 2
    width = half // PARTS
    total = PARTS * tokens
    slots = 2 * CAP
    for part in range(PARTS):
        stacked[part * tokens:(part + 1) * tokens, :] = state[:, part * width:(part + 1) * width]
    expert = me[0] ^ iota((8, total), 0)
    chosen = table[4 * turn:4 * turn + 2, :].astype(jnp.int32)
    named = (chosen[0:1, :] == expert) | (chosen[1:2, :] == expert)
    earlier = (iota((total, total), 0) // rows == iota((total, total), 1) // rows) & (
        iota((total, total), 0) < iota((total, total), 1)
    )
    before = matmul(ones_where(named), ones_where(earlier))
    column = iota((8, total), 1)
    start = column // tokens * slots + column // rows % 2 * CAP
    place = jnp.where(named, start + before.astype(jnp.int32), -1)
    for apart in range(EXPERTS):
        hit = iota((PARTS * slots, total), 0) == place[apart:apart + 1, :]
        outs[apart][...] = matmul(ones_where(hit), stacked[...]).astype(jnp.bfloat16)


def enter_kernel(turn, me, kept, other, table, o0, o1, o2, o3, state, stacked):
    joined(me, kept, other, state)
    packed(me, state, table, turn, (o0, o1, o2, o3), stacked)


def relay_kernel(turn, edge, me, moved, moved_rest, kept, other, table, o0, o1, o2, o3, state, stacked):
    state[:moved.shape[0], :] = moved[...]
    state[moved.shape[0]:, :] = moved_rest[...]

    @pl.when(me[2 + edge] == 1)
    def _():
        joined(me, kept, other, state)

    packed(me, state, table, turn, (o0, o1, o2, o3), stacked)


def pack_shapes(rows, half):
    width = half // PARTS
    outs = [bf16(PARTS * 2 * CAP, width)] * EXPERTS + [bf16(2 * rows, half)]
    return outs, [pltpu.VMEM((PARTS * 2 * rows, width), jnp.bfloat16)]


def enter(me, turn, kept, other, table, after):
    outs, scratch = pack_shapes(*other.shape)
    made = call(functools.partial(enter_kernel, turn), "enter", outs, me, kept, other, table, after=after, scratch=scratch)
    return made[:EXPERTS], made[EXPERTS]


def relay(me, turn, edge, moved, kept, other, table):
    outs, scratch = pack_shapes(*other.shape)
    kernel = functools.partial(relay_kernel, turn, edge)
    made = call(kernel, "relay", outs, me, *moved, kept, other, table, scratch=scratch)
    return made[:EXPERTS], made[EXPERTS]


def load_kernel(me, source, unread, out, done):
    copy = pltpu.make_async_copy(source, out, done.at[0])
    copy.start()
    copy.wait()


def load(me, weight, after):
    return pl.pallas_call(
        load_kernel,
        out_shape=bf16(*weight.shape),
        in_specs=[
            pl.BlockSpec(memory_space=pltpu.SMEM),
            pl.BlockSpec(memory_space=pltpu.HBM),
            pl.BlockSpec(memory_space=pl.ANY),
        ],
        out_specs=whole(1)[0],
        scratch_shapes=[pltpu.SemaphoreType.DMA((1,))],
        compiler_params=pltpu.CompilerParams(vmem_limit_bytes=LIMIT),
        cost_estimate=pl.CostEstimate(flops=0, bytes_accessed=0, transcendentals=0),
        name="load",
    )(me, weight, after)


def first_kernel(me, r0, r1, r2, r3, gain, weight, gates, ups, rows_out, squares):
    slots = 2 * CAP
    block, width = r0.shape
    units = weight.shape[1] // 4
    held = [ref[...].astype(jnp.float32) for ref in (r0, r1, r2, r3)]
    total = jnp.zeros((block, 1), jnp.float32)
    for part in range(PARTS):
        values = jnp.concatenate([rows[part * slots:(part + 1) * slots, :] for rows in held], axis=0)
        total = total + jnp.sum(values * values, axis=1, keepdims=True)
        start = pl.multiple_of(me[1] * PARTS * width + part * width, width)
        scaled = values * gain[:, pl.ds(start, width)]
        rows_out[:, part * width:(part + 1) * width] = scaled.astype(jnp.bfloat16)
    squares[...] = jnp.broadcast_to(total, squares.shape)
    lane = iota(squares.shape, 1)
    high, middle, low = [piece.astype(jnp.float32) for piece in pieces(total)]
    sent = jnp.where(lane == 0, high, jnp.where(lane == 1, middle, jnp.where(lane == 2, low, 0.0)))
    turned = lax.dot_general(
        sent.astype(jnp.bfloat16),
        ones_where(iota((block, block), 0) == iota((block, block), 1)),
        (((0,), (0,)), ((), ())),
        preferred_element_type=jnp.float32,
    )
    extra = gates.shape[0] - block
    gates[block:, :] = jnp.zeros((extra, units), jnp.bfloat16)
    gates[block:, :block] = turned[:extra, :].astype(jnp.bfloat16)
    for kind in range(2):
        start = pl.multiple_of(units * (2 * kind + 1 - me[1]), units)
        columns = matmul(rows_out[...], weight[:, pl.ds(start, units)]).astype(jnp.bfloat16)
        (gates, ups)[kind][:block, :] = columns


def first(me, received, gain, weight, after):
    block, width = received[0].shape
    half, both = weight.shape
    outs = [bf16(block + 16, both // 4), bf16(block, both // 4), bf16(block, half), f32(block, 128)]
    return call(first_kernel, "first", outs, me, *received, gain, weight, after=after)


def own_kernel(me, rows_in, weight, own):
    units = weight.shape[1] // 4
    for kind in range(2):
        start = pl.multiple_of(units * (2 * kind + me[1]), units)
        own[:, kind * units:(kind + 1) * units] = matmul(rows_in[...], weight[:, pl.ds(start, units)])


def own_half(me, rows_in, weight):
    return call(own_kernel, "own", f32(rows_in.shape[0], weight.shape[1] // 2), me, rows_in, weight)


def act_kernel(model_width, me, own, gates, ups, squares, h0, h1):
    block, both = own.shape
    units = both // 2
    pair = lax.dot_general(
        ones_where(iota((block, block), 0) == iota((block, block), 1)),
        gates[block:, :block],
        (((1,), (1,)), ((), ())),
        preferred_element_type=jnp.float32,
    )
    mean = (squares[:, 0:1] + ((pair[:, 2:3] + pair[:, 1:2]) + pair[:, 0:1])) / model_width
    scale = lax.rsqrt(mean + EPSILON)
    gate = (own[:, :units] + gates[:block, :].astype(jnp.float32)) * scale
    up = (own[:, units:] + ups[...].astype(jnp.float32)) * scale
    hidden = (gate / (1.0 + jnp.exp(-gate)) * up).astype(jnp.bfloat16)
    h0[...] = hidden[:, :units // 2]
    h1[...] = hidden[:, units // 2:]


def act(me, own, gates, ups, squares, model_width):
    block, both = own.shape
    outs = [bf16(block, both // 4)] * 2
    return call(functools.partial(act_kernel, model_width), "act", outs, me, own, gates, ups, squares)


def third_kernel(me, h0, h1, t0, t1, weight, o0, o1, o2, o3, hidden):
    slots = 2 * CAP
    block, units = hidden.shape
    size = units // 4
    width = o0.shape[1]
    for index, pair in enumerate(((h0, h1), (t0, t1))):
        for place, ref in enumerate(pair):
            start = ((me[1] ^ index) * 2 + place) * size
            hidden[:, pl.ds(pl.multiple_of(start, size), size)] = ref[...]
    results = []
    for part in range(PARTS):
        columns = slice(part * width, (part + 1) * width)
        results.append(matmul(hidden[...], weight[:, columns]))
    for apart, out in enumerate((o0, o1, o2, o3)):
        rows = [result[apart * slots:(apart + 1) * slots, :] for result in results]
        out[...] = jnp.concatenate(rows, axis=0).astype(jnp.bfloat16)


def third(me, hidden, hidden_other, weight):
    block = hidden[0].shape[0]
    units, half = weight.shape
    outs = [bf16(block, half // PARTS)] * EXPERTS
    scratch = [pltpu.VMEM((block, units), jnp.bfloat16)]
    return call(third_kernel, "third", outs, me, *hidden, *hidden_other, weight, scratch=scratch)


def spread_gates(me, table, turn, rows, start):
    total = table.shape[0]
    slots = 2 * CAP
    expert = me[0] ^ iota((total, 128), 1)
    chosen = table[:, 4 * turn:4 * turn + 2].astype(jnp.int32)
    share = table[:, 4 * turn + 2:4 * turn + 4]
    hits = [chosen[:, k:k + 1] == expert for k in range(2)]
    weight = jnp.where(hits[0], share[:, 0:1], 0.0) + jnp.where(hits[1], share[:, 1:2], 0.0)
    named = hits[0] | hits[1]
    earlier = (iota((total, total), 0) // rows == iota((total, total), 1) // rows) & (
        iota((total, total), 0) > iota((total, total), 1)
    )
    before = matmul(ones_where(earlier), ones_where(named))
    place = jnp.where(named, start + before.astype(jnp.int32), -1)
    spreads = []
    for apart in range(EXPERTS):
        hit = iota((total, PARTS * slots), 1) == place[:, apart:apart + 1]
        spreads.append(jnp.where(hit, weight[:, apart:apart + 1], 0.0))
    return spreads


def combined(spreads, received):
    mixed = jnp.zeros((spreads[0].shape[0], received[0].shape[1]), jnp.float32)
    for spread, ref in zip(spreads, received):
        high = spread.astype(jnp.bfloat16)
        low = (spread - high.astype(jnp.float32)).astype(jnp.bfloat16)
        mixed = mixed + matmul(high, ref[...]) + matmul(low, ref[...])
    return mixed


def mixed_parts(me, table, turn, received, tokens):
    rows = tokens // 2
    line = iota((PARTS * tokens, 128), 0)
    start = line // tokens * 2 * CAP + line // rows % 2 * CAP
    return combined(spread_gates(me, table, turn, rows, start), received)


def mix_kernel(turn, me, state, table, r0, r1, r2, r3, out):
    tokens = state.shape[0]
    width = r0.shape[1]
    mixed = mixed_parts(me, table, turn, (r0, r1, r2, r3), tokens)
    for part in range(PARTS):
        span = slice(part * width, (part + 1) * width)
        summed = state[:, span].astype(jnp.float32) + mixed[part * tokens:(part + 1) * tokens, :]
        out[:, span] = summed.astype(jnp.bfloat16)


def halves_kernel(turn, me, state, table, *refs):
    *received, upper, lower, result = refs
    mix_kernel(turn, me, state, table, *received, result)
    upper[...] = result[:upper.shape[0], :]
    lower[...] = result[upper.shape[0]:, :]


def mix(me, turn, state, table, received, after):
    kernel = functools.partial(halves_kernel, turn)
    tokens, half = state.shape
    outs = [bf16(tokens // 2, half)] * 2
    scratch = [pltpu.VMEM(state.shape, jnp.bfloat16)]
    return call(kernel, "mix", outs, me, state, table, *received, after=after, scratch=scratch)


def last_kernel(turn, side, me, state, table, r0, r1, r2, r3, out, lines):
    rows, half = out.shape
    width = r0.shape[1]
    slots = 2 * CAP
    total = PARTS * rows
    source = me[1] ^ side
    for part in range(PARTS):
        start = pl.multiple_of((2 * part + source) * rows, rows)
        lines[part * rows:(part + 1) * rows, :] = table[pl.ds(start, rows), :]
    spreads = spread_gates(me, lines, turn, rows, iota((total, 128), 0) // rows * slots + source * CAP)
    mixed = combined(spreads, (r0, r1, r2, r3))
    start = pl.multiple_of(source * rows, rows)
    for part in range(PARTS):
        span = slice(part * width, (part + 1) * width)
        values = state[pl.ds(start, rows), span].astype(jnp.float32)
        out[:, span] = (values + mixed[part * rows:(part + 1) * rows, :]).astype(jnp.bfloat16)


def last(me, turn, side, state, table, received, after):
    tokens, half = state.shape
    rows = tokens // 2
    scratch = [pltpu.VMEM((PARTS * rows, table.shape[1]), jnp.float32)]
    kernel = functools.partial(last_kernel, turn, side)
    return call(kernel, "last", bf16(rows, half), me, state, table, *received, after=after, scratch=scratch)


def finish_kernel(me, kept, other, out):
    half = kept.shape[1]
    out[:, pl.ds(pl.multiple_of(me[1] * half, half), half)] = kept[...]
    out[:, pl.ds(pl.multiple_of((1 - me[1]) * half, half), half)] = other[...]


def finish(me, kept, other):
    return call(finish_kernel, "finish", bf16(kept.shape[0], 2 * kept.shape[1]), me, kept, other)


def along(block, apart):
    return lax.ppermute(block, "expert", [(i, i ^ 2 * apart) for i in range(lax.axis_size("expert"))])


def across(blocks, behind=None, hold=False):
    own, near, two, three = blocks
    if behind is not None:
        two, three, *behind[2:] = lax.optimization_barrier((two, three, *behind[2:]))
        near, behind[1] = lax.optimization_barrier((near, behind[1]))
    return [own, along(near, 1), along(two, 2), three if hold else along(three, 3)]


def paired_shards(
    east_batch,
    west_batch,
    east_entering,
    west_entering,
    east_experts,
    west_experts,
    east_gates,
    west_gates,
    norm_gain,
    expert_in,
    expert_down,
):
    section_index = lax.axis_index("pipe")
    section_count = lax.axis_size("pipe")
    member = lax.axis_index("expert")
    edges = [section_index == 0, section_index == section_count - 1]
    me = jnp.stack([member // 2, member % 2, *edges]).astype(jnp.int32)
    rows, model_width = east_batch.shape[1:]
    kinds = [
        jnp.swapaxes(array[tick, 0], 0, 1).astype(jnp.float32)
        for experts, gates in ((east_experts, east_gates), (west_experts, west_gates))
        for tick in range(TICKS)
        for array in (experts, gates)
    ]
    lists = jnp.concatenate(kinds, axis=0)

    batches = [east_batch[0], west_batch[0]]
    entering = [east_entering[0], west_entering[0]]
    east_halves = cut(me, batches[:1])[0]
    as_rows, as_columns = tables(me, lists, partner(lists, "expert", 0))
    east_halves = crossed(east_halves)
    moved = [None, None]
    results = [None, None]
    states = [None, None]
    ahead = None
    for tick in range(TICKS):
        final = tick + 1 == TICKS
        arrived = [None, None]
        for stream in range(2):
            turn = stream * TICKS + tick
            if tick == 0:
                after, west_halves = [], None
                if stream == 1:
                    west_halves = crossed(cut(me, batches[1:], [states[0]])[0])
                    entering_halves = [crossed(halves) for halves in cut(me, entering, [west_halves[0]])]
                    weight_in = load(me, expert_in[0, 0], states[0])
                    weight_out = expert_down[0, 0]
                    after = [weight_in]
                sent, states[stream] = enter(me, turn, *(east_halves, west_halves)[stream], as_rows, after)
            else:
                sent, states[stream] = relay(
                    me, turn, stream, moved[stream], *entering_halves[stream], as_rows
                )
                if stream == 0:
                    pieces_now = mix(me, turn_before, state_before, as_columns, ahead, [sent[0]])
                    moved[1] = [shifted(piece, "pipe", -1) for piece in pieces_now]
            arrived[stream] = across(sent, ahead, stream == 1)
            ahead = arrived[stream]
        behind = states[1]
        crossings = [halves[1] for halves in entering_halves] if tick == 0 else []
        for stream in range(2):
            turn = stream * TICKS + tick
            gates, ups, scaled, squares = first(me, arrived[stream], norm_gain, weight_in, [behind, *crossings])
            crossings = []
            held = arrived[1 - stream]
            scaled, held[3] = lax.optimization_barrier((scaled, held[3]))
            held[3] = along(held[3], 3)
            gates, ups = partner(gates, "expert", 0), partner(ups, "expert", 0)
            own = own_half(me, scaled, weight_in)
            hidden = act(me, own, gates, ups, squares, model_width)
            result = third(me, hidden, [partner(half, "expert", 0) for half in hidden], weight_out)
            behind = result[0]
            arrived[stream] = across(result, ahead, stream == 0)
            ahead = arrived[stream]
        if final:
            for stream in range(2):
                turn = stream * TICKS + tick
                sent = last(me, turn, 1, states[stream], as_columns, arrived[stream], [behind])
                other = partner(sent, "expert", 0)
                kept = last(me, turn, 0, states[stream], as_columns, arrived[stream], [sent])
                results[stream] = finish(me, kept, other)
        else:
            pieces_now = mix(me, tick, states[0], as_columns, arrived[0], [behind])
            moved[0] = [shifted(piece, "pipe", 1) for piece in pieces_now]
            turn_before, state_before = TICKS + tick, states[1]
    return (results[0][None], results[1][None])


def solution(mesh):
    in_specs = (
        P("pipe", "expert", None),
        P("pipe", "expert", None),
        P(None, "expert", None),
        P(None, "expert", None),
        P(None, "pipe", "expert", None),
        P(None, "pipe", "expert", None),
        P(None, "pipe", "expert", None),
        P(None, "pipe", "expert", None),
        P("pipe", None),
        P("pipe", "expert", None, None),
        P("pipe", "expert", None, None),
    )
    out_specs = (P("pipe", "expert", None), P("pipe", "expert", None))
    groups = mesh.shape["expert"] // EXPERTS
    shards = paired_shards if groups == 2 else general_shards
    return jax.shard_map(shards, mesh=mesh, in_specs=in_specs, out_specs=out_specs, check_vma=False)
```
